32 devices in a mesh: chain: 4 (over y, core), col: 8 (over z, x).
Axes of the slice: x: 2, y: 2, z: 4, core: 2. Of those that a mesh axis runs over, the one named last changes fastest.
Arguments:
- sources: float32 [4, 32, 64, 128], P('chain', 'col'), may hold values from -6 to 6
- diag_inverse: float32 [4, 32, 128, 128], P('chain', 'col')
- factor_tiles: float32 [4, 752, 128, 128], P('chain', 'col'), may hold values from -0.109375 to 0.109375
- tile_rows: int32 [4, 752], P('chain', 'col'), may hold values from 0 to 31
- tile_cols: int32 [4, 752], P('chain', 'col'), may hold values from 0 to 31, as said below
Outputs:
- solved: float32 [4, 32, 64, 128], P('chain', 'col')
- leaving: float32 [4, 32, 64, 128], P('chain', 'col')
The draws below stay inside these ranges and needn't reach their ends.
Inputs may be any that keep to these rules, and one draw needn't show every extreme that they name: `tile_cols`: entries 94 * c to 94 * (c + 1) - 1 of a group name tile columns 4 * c to 4 * (c + 1) - 1.
All inputs are finite; a program needn't handle non-finite values.
Results may differ from the reference program's by a relative error of at most 0.00018.
Values sent between devices are 32-bit elements; how exact they have to be, the bound alone decides.
A program may use at most 64 MiB of HBM per device.

```python
import jax
import jax.numpy as jnp
from jax import lax

TILE = 128
SRC = 64
TPD = 4
NOFF = 94
GROUPS = 4
NT = 32
OFFALL = 752
FAN = 3008


def draw_diag_inverse(key, part):
    first = jax.random.fold_in(key, 11)
    second = jax.random.fold_in(key, 12)
    diag_values = jnp.exp(jax.random.uniform(first, (GROUPS, NT, TILE), jnp.float32, jnp.log(0.5), jnp.log(2.0)))
    off_part = jax.random.normal(second, (GROUPS, NT, TILE, TILE), jnp.float32) * (0.35 / jnp.sqrt(TILE * 1.0))
    eye_mat = jnp.eye(TILE, dtype=jnp.float32)
    matrix = off_part + diag_values[..., None] * eye_mat
    return matrix


def draw_tile_cols(key, part):
    picks = jax.random.randint(jax.random.fold_in(key, 21), (GROUPS, OFFALL), 0, TPD)
    blocks = jnp.arange(OFFALL, dtype=jnp.int32) // NOFF
    return (blocks[None, :] * TPD + picks).astype(jnp.int32)


def with_ends(drawn, key, smallest, high):
    index_at = [jax.random.randint(jax.random.fold_in(key, axis), (), 0, length) for axis, length in enumerate(drawn.shape)]
    longest = drawn.shape.index(max(drawn.shape))
    beside = index_at[:longest] + [(index_at[longest] + 1) % drawn.shape[longest]] + index_at[longest + 1:]
    return drawn.at[tuple(index_at)].set(smallest).at[tuple(beside)].set(high)


def shard_levels(stream_key, shape, split, smallest, high):
    loudness = 1.0
    for axis_at, blocks in split:
        draws = jax.random.uniform(jax.random.fold_in(jax.random.fold_in(stream_key, 6), axis_at), (blocks,), jnp.float32, smallest / len(split), high / len(split))
        loudness = loudness * jnp.repeat(jnp.exp(draws), shape[axis_at] // blocks).reshape((-1,) + (1,) * (len(shape) - 1 - axis_at))
    return loudness


def centred(rng, extent, deviation, most, pieces=(), kind=jnp.bfloat16):
    gain = shard_levels(rng, extent, pieces, -0.22, 0.18) if pieces else 1.0
    drawn = jax.random.normal(rng, extent, jnp.float32) * deviation * gain
    return jnp.minimum(jnp.maximum(drawn, -most), most).astype(kind)


def setup_inputs(seed: int = 0) -> dict:
    key_list = jax.random.split(jax.random.key(seed), 6)
    sources = centred(key_list[0], (GROUPS, NT, SRC, TILE), 1.0, 6.0, ((0, 4), (1, 8)), jnp.float32)
    diag_inverse = draw_diag_inverse(jax.random.fold_in(key_list[5], 71), 0)
    factor_tiles = centred(key_list[2], (GROUPS, OFFALL, TILE, TILE), FAN ** -0.5, 0.109375, ((0, 4), (1, 8)), jnp.float32)
    tile_rows = with_ends(jax.random.randint(key_list[3], (GROUPS, OFFALL), 0, NT), jax.random.fold_in(key_list[3], 1), 0, NT - 1).astype(jnp.int32)
    tile_cols = draw_tile_cols(jax.random.fold_in(key_list[5], 71), 0)
    return {"sources": sources, "diag_inverse": diag_inverse, "factor_tiles": factor_tiles, "tile_rows": tile_rows, "tile_cols": tile_cols}


def reference(sources, diag_inverse, factor_tiles, tile_rows, tile_cols):
    highest = lax.Precision.HIGHEST
    inbound = jnp.zeros((NT, SRC, TILE), jnp.float32)
    solved_list = []
    leaving_list = []
    for group in range(GROUPS):
        right_side = sources[group] - inbound
        current = jnp.einsum("trc,tsc->tsr", diag_inverse[group], right_side, precision=highest)
        picked = jnp.take(current, tile_cols[group].astype(jnp.int32), axis=0)
        products = jnp.einsum("krc,ksc->ksr", factor_tiles[group], picked, precision=highest)
        onehot = (tile_rows[group][:, None] == jnp.arange(NT, dtype=jnp.int32)[None, :]).astype(jnp.float32)
        inbound = jnp.einsum("kt,ksr->tsr", onehot, products, precision=highest)
        solved_list.append(current)
        leaving_list.append(inbound)
    return jnp.stack(solved_list), jnp.stack(leaving_list)
```

```python
import functools

import jax
import jax.numpy as jnp
from jax import lax
from jax.experimental import pallas as pl
from jax.experimental.pallas import tpu as pltpu
from jax.sharding import PartitionSpec as P

MESH = pl.DeviceIdType.MESH
MIB = 1 << 20


def split(value):
    high = value.astype(jnp.bfloat16)
    low = (value - high.astype(jnp.float32)).astype(jnp.bfloat16)
    return high, low


def times_transposed(left, right):
    return lax.dot_general(left, right, (((1,), (1,)), ((), ())), preferred_element_type=jnp.float32)


def merge_kernel(chunk, tiles, rows_ref, cols_ref, factor_ref, high_ref, low_ref, total):
    step = pl.program_id(0)
    size = factor_ref.shape[-1]
    width = high_ref.shape[-1] // size
    blocks = high_ref.shape[0] // size

    @pl.when(step == 0)
    def _():
        def clear(block, carry):
            at = pl.ds(pl.multiple_of(block * size, size), size)
            total[at, :] = jnp.zeros((size, total.shape[1]), jnp.float32)
            return carry

        lax.fori_loop(0, blocks, clear, 0)

    def add(j, carry):
        k = step * chunk + j
        row = pl.ds(pl.multiple_of(rows_ref[k] * size, size), size)
        col = pl.ds(pl.multiple_of(cols_ref[k] * size, size), size)
        total[row, col] += factor_ref[j]
        return carry

    lax.fori_loop(0, jnp.minimum(chunk, tiles - step * chunk), add, 0)

    @pl.when(step == pl.num_programs(0) - 1)
    def _():
        def finish(block, carry):
            at = pl.ds(pl.multiple_of(block * size, size), size)
            for c in range(width):
                cs = slice(c * size, (c + 1) * size)
                high, low = split(total[at, cs])
                high_ref[at, cs] = high
                low_ref[at, cs] = low
            return carry

        lax.fori_loop(0, blocks, finish, 0)


def merge(factor, rows, cols, row_tiles, col_tiles):
    tiles, size, _ = factor.shape
    chunk = 16
    shape = (row_tiles * size, col_tiles * size)
    whole = pl.BlockSpec(memory_space=pltpu.VMEM)
    return pl.pallas_call(
        functools.partial(merge_kernel, chunk, tiles),
        out_shape=[pltpu.VMEM(shape, jnp.bfloat16)] * 2,
        grid_spec=pltpu.PrefetchScalarGridSpec(
            num_scalar_prefetch=2,
            grid=(pl.cdiv(tiles, chunk),),
            in_specs=[pl.BlockSpec((chunk, size, size), lambda i, *_: (i, 0, 0))],
            out_specs=[whole] * 2,
            scratch_shapes=[pltpu.VMEM(shape, jnp.float32)],
        ),
        compiler_params=pltpu.CompilerParams(
            dimension_semantics=("arbitrary",), vmem_limit_bytes=24 * MIB + 2 * shape[0] * shape[1]
        ),
    )(rows, cols, factor)


def chain_kernel(
    groups, nx, nz,
    src_ref, inv_ref, high_ref, low_ref, solved_ref, leaving_ref,
    panel, own, xout, xin, zout, zin, zlast, bout, bin_,
    xsend, xrecv, zsend, zrecv, lrecv, bsend, brecv,
):
    g = lax.axis_index("chain")
    col = lax.axis_index("col")
    x = lax.rem(col, nx)
    z = lax.div(col, nx)
    per, sources, size = src_ref.shape
    last = g == groups - 1

    def place(dx, dz):
        return lax.rem(z + dz, nz) * nx + lax.rem(x + dx, nx)

    barrier = pltpu.get_barrier_semaphore()

    def greet(chain, dx, dz):
        pl.semaphore_signal(barrier, inc=1, device_id=(chain, place(dx, dz)), device_id_type=MESH)

    for dx in range(1, nx):
        greet(g, dx, 0)

    @pl.when(g > 0)
    def _():
        for dz in range(nz):
            greet(g - 1, 0, dz)

    @pl.when(jnp.logical_not(last))
    def _():
        for dz in range(nz):
            greet(g + 1, 0, dz)

    @pl.when(last)
    def _():
        for dz in range(1, nz):
            greet(g, 0, dz)

    awaited = (nx - 1) + jnp.where(g > 0, nz, 0) + jnp.where(last, nz - 1, nz)
    pl.semaphore_wait(barrier, awaited)

    def x_copy(dx, dz):
        return pltpu.make_async_remote_copy(
            src_ref=xout.at[dx - 1, dz], dst_ref=xin.at[dx - 1, dz],
            send_sem=xsend.at[dx - 1, dz], recv_sem=xrecv.at[dx - 1, dz],
            device_id=(g, place(dx, 0)), device_id_type=MESH,
        )

    def z_copy(dz):
        return pltpu.make_async_remote_copy(
            src_ref=zout.at[dz], dst_ref=zin.at[dz],
            send_sem=zsend.at[dz], recv_sem=zrecv.at[dz],
            device_id=(g + 1, place(0, dz)), device_id_type=MESH,
        )

    def last_copy(dz):
        return pltpu.make_async_remote_copy(
            src_ref=zout.at[dz], dst_ref=zlast.at[dz],
            send_sem=zsend.at[dz], recv_sem=lrecv.at[dz],
            device_id=(g, place(0, dz)), device_id_type=MESH,
        )

    back = pltpu.make_async_remote_copy(
        src_ref=bout, dst_ref=bin_, send_sem=bsend, recv_sem=brecv,
        device_id=(g - 1, col), device_id_type=MESH,
    )

    @pl.when(g == 0)
    def _():
        bout[...] = jnp.zeros(bout.shape, jnp.float32)

    @pl.when(g > 0)
    def _():
        for dz in range(nz):
            z_copy(dz).wait_recv()
        total = zin[0]
        for dz in range(1, nz):
            total = total + zin[dz]
        bout[...] = total
        back.start()

    for t in range(per):
        right, rest = split(src_ref[t] - bout[t])
        inv, inv_rest = split(inv_ref[t])
        both = times_transposed(jnp.concatenate([right, rest], axis=0), inv)
        current = both[:sources] + both[sources:] + times_transposed(right, inv_rest)
        solved_ref[t] = current
        high, low = split(current)
        panel[:sources, t * size:(t + 1) * size] = high
        panel[sources:, t * size:(t + 1) * size] = low

    def chunk(dx, dz, store):
        rows = per * size
        at = pl.ds(pl.multiple_of(place(dx, dz) * rows, rows), rows)
        both = times_transposed(panel[...], high_ref[at, :])
        result = both[:sources] + both[sources:] + times_transposed(panel[:sources, :], low_ref[at, :])
        for t in range(per):
            store[t] = result[:, t * size:(t + 1) * size]

    order = sorted(range(1, nz), key=lambda d: abs(2 * d - nz)) + [0]
    for dz in order:
        for dx in range(1, nx):
            chunk(dx, dz, xout.at[dx - 1, dz])
            x_copy(dx, dz).start()
    for dz in order:
        chunk(0, dz, own.at[dz])
    for dz in order:
        for dx in range(1, nx):
            x_copy(dx, dz).wait_recv()
        for t in range(per):
            part = own[dz, t]
            for dx in range(1, nx):
                part = part + xin[dx - 1, dz, t]
            zout[dz, t] = part

        @pl.when(jnp.logical_not(last))
        def _():
            z_copy(dz).start()

        if dz > 0:
            @pl.when(last)
            def _():
                last_copy(dz).start()

    @pl.when(last)
    def _():
        for dz in range(1, nz):
            last_copy(dz).wait_recv()
        total = zout[0]
        for dz in range(1, nz):
            total = total + zlast[dz]
        leaving_ref[...] = total
        for dz in range(1, nz):
            last_copy(dz).wait_send()

    @pl.when(jnp.logical_not(last))
    def _():
        back.wait_recv()
        leaving_ref[...] = bin_[...]
        for dz in range(nz):
            z_copy(dz).wait_send()

    for dz in order:
        for dx in range(1, nx):
            x_copy(dx, dz).wait_send()

    @pl.when(g > 0)
    def _():
        back.wait_send()


def local(nx, groups, col_devices, sources, diag_inverse, factor_tiles, tile_rows, tile_cols):
    per, panel_sources, size = sources.shape[1:]
    nz = col_devices // nx
    local_cols = tile_cols[0] - lax.axis_index("col") * per
    high, low = merge(factor_tiles[0], tile_rows[0], local_cols, per * col_devices, per)
    block = (per, panel_sources, size)
    whole = pl.BlockSpec(memory_space=pltpu.VMEM)
    dma = pltpu.SemaphoreType.DMA
    solved, leaving = pl.pallas_call(
        functools.partial(chain_kernel, groups, nx, nz),
        out_shape=[jax.ShapeDtypeStruct(block, jnp.float32)] * 2,
        in_specs=[whole] * 4,
        out_specs=[whole] * 2,
        scratch_shapes=[
            pltpu.VMEM((2 * panel_sources, per * size), jnp.bfloat16),
            pltpu.VMEM((nz,) + block, jnp.float32),
            pltpu.VMEM((nx - 1, nz) + block, jnp.float32),
            pltpu.VMEM((nx - 1, nz) + block, jnp.float32),
            pltpu.VMEM((nz,) + block, jnp.float32),
            pltpu.VMEM((nz,) + block, jnp.float32),
            pltpu.VMEM((nz,) + block, jnp.float32),
            pltpu.VMEM(block, jnp.float32),
            pltpu.VMEM(block, jnp.float32),
            dma((nx - 1, nz)),
            dma((nx - 1, nz)),
            dma((nz,)),
            dma((nz,)),
            dma((nz,)),
            dma(()),
            dma(()),
        ],
        compiler_params=pltpu.CompilerParams(
            collective_id=0, has_side_effects=True, vmem_limit_bytes=36 * MIB
        ),
    )(sources[0], diag_inverse[0], high, low)
    return (solved[None], leaving[None])


def solution(mesh):
    groups, col_devices = mesh.shape["chain"], mesh.shape["col"]
    nx = max(d for d in range(1, col_devices + 1) if col_devices % d == 0 and d * d <= col_devices)
    return jax.shard_map(
        functools.partial(local, nx, groups, col_devices),
        mesh=mesh,
        in_specs=(
            P("chain", "col", None, None),
            P("chain", "col", None, None),
            P("chain", "col", None, None),
            P("chain", "col"),
            P("chain", "col"),
        ),
        out_specs=(P("chain", "col", None, None), P("chain", "col", None, None)),
        check_vma=False,
    )
```

```python
import functools

import jax
import jax.numpy as jnp
from jax import lax
from jax.experimental import pallas as pl
from jax.experimental.pallas import tpu as pltpu
from jax.sharding import PartitionSpec as P

MESH = pl.DeviceIdType.MESH
MIB = 1 << 20
PANELS = 4


def split(value):
    high = value.astype(jnp.bfloat16)
    low = (value - high.astype(jnp.float32)).astype(jnp.bfloat16)
    return high, low


def times_transposed(left, right):
    return lax.dot_general(left, right, (((1,), (1,)), ((), ())), preferred_element_type=jnp.float32)


def merge_kernel(pieces, rows_ref, cols_ref, factor_ref, high_ref, low_ref, held, total, arrived):
    tiles, size, _ = factor_ref.shape
    width = high_ref.shape[1] // size
    blocks = high_ref.shape[0] // size

    def fetch(i):
        span = pl.ds(pieces[i], pieces[i + 1] - pieces[i])
        return pltpu.make_async_copy(factor_ref.at[span], held.at[span], arrived.at[i])

    for i in range(len(pieces) - 1):
        fetch(i).start()

    def clear(block, carry):
        at = pl.ds(pl.multiple_of(block * size, size), size)
        total[at, :] = jnp.zeros((size, total.shape[1]), jnp.float32)
        return carry

    lax.fori_loop(0, blocks, clear, 0)

    def add(k, carry):
        row = pl.ds(pl.multiple_of(rows_ref[0, k] * size, size), size)
        col = pl.ds(pl.multiple_of(lax.rem(cols_ref[0, k], width) * size, size), size)
        total[row, col] += held[k]
        return carry

    for i in range(len(pieces) - 1):
        fetch(i).wait()
        lax.fori_loop(pieces[i], pieces[i + 1], add, 0)

    def finish(block, carry):
        at = pl.ds(pl.multiple_of(block * size, size), size)
        for c in range(width):
            cs = slice(c * size, (c + 1) * size)
            high, low = split(total[at, cs])
            high_ref[at, cs] = high
            low_ref[at, cs] = low
        return carry

    lax.fori_loop(0, blocks, finish, 0)


def merge(factor, rows, cols, row_tiles, col_tiles):
    tiles, size, _ = factor.shape
    pieces = list(range(0, tiles, 16)) + [tiles]
    shape = (row_tiles * size, col_tiles * size)
    whole = pl.BlockSpec(memory_space=pltpu.VMEM)
    scalars = pl.BlockSpec(memory_space=pltpu.SMEM)
    return pl.pallas_call(
        functools.partial(merge_kernel, pieces),
        out_shape=[pltpu.VMEM(shape, jnp.bfloat16)] * 2,
        in_specs=[scalars, scalars, pl.BlockSpec(memory_space=pltpu.HBM)],
        out_specs=[whole] * 2,
        scratch_shapes=[
            pltpu.VMEM(factor.shape, jnp.float32),
            pltpu.VMEM(shape, jnp.float32),
            pltpu.SemaphoreType.DMA((len(pieces) - 1,)),
        ],
        compiler_params=pltpu.CompilerParams(vmem_limit_bytes=40 * MIB),
    )(*(pltpu.with_memory_space_constraint(a, pltpu.HBM) for a in (rows, cols, factor)))


def chain_kernel(
    groups, nx, nz, panels,
    src_ref, inv_ref, high_ref, low_ref, solved_ref, leaving_ref,
    inv_high, inv_low, operand, own, xout, xin, zout, zin, zlast, bout, bin_,
    xsend, xrecv, zsend, zrecv, lrecv, bsend, brecv,
):
    g = lax.axis_index("chain")
    col = lax.axis_index("col")
    x = lax.rem(col, nx)
    z = lax.div(col, nx)
    per, sources, size = src_ref.shape
    wide = sources // panels
    last = g == groups - 1
    inner = jnp.logical_not(last)

    def place(dx, dz):
        return lax.rem(z + dz, nz) * nx + lax.rem(x + dx, nx)

    barrier = pltpu.get_barrier_semaphore()

    def greet(chain, dx, dz):
        pl.semaphore_signal(barrier, inc=1, device_id=(chain, place(dx, dz)), device_id_type=MESH)

    for dx in range(1, nx):
        greet(g, dx, 0)

    @pl.when(g > 0)
    def _():
        for dz in range(nz):
            greet(g - 1, 0, dz)

    @pl.when(inner)
    def _():
        for dz in range(nz):
            greet(g + 1, 0, dz)

    @pl.when(last)
    def _():
        for dz in range(1, nz):
            greet(g, 0, dz)

    for t in range(per):
        inv_high[t], inv_low[t] = split(inv_ref[t])

    @pl.when(g == 0)
    def _():
        bout[...] = jnp.zeros(bout.shape, jnp.float32)

    awaited = (nx - 1) + jnp.where(g > 0, nz, 0) + jnp.where(last, nz - 1, nz)
    pl.semaphore_wait(barrier, awaited)

    def x_copy(p, dx, dz):
        return pltpu.make_async_remote_copy(
            src_ref=xout.at[p, dx - 1, dz], dst_ref=xin.at[p, dx - 1, dz],
            send_sem=xsend.at[p, dx - 1, dz], recv_sem=xrecv.at[p, dx - 1, dz],
            device_id=(g, place(dx, 0)), device_id_type=MESH,
        )

    def z_copy(p, dz):
        return pltpu.make_async_remote_copy(
            src_ref=zout.at[p, dz], dst_ref=zin.at[p, dz],
            send_sem=zsend.at[p, dz], recv_sem=zrecv.at[p, dz],
            device_id=(g + 1, place(0, dz)), device_id_type=MESH,
        )

    def last_copy(p, dz):
        return pltpu.make_async_remote_copy(
            src_ref=zout.at[p, dz], dst_ref=zlast.at[p, dz],
            send_sem=zsend.at[p, dz], recv_sem=lrecv.at[p, dz],
            device_id=(g, place(0, dz)), device_id_type=MESH,
        )

    def back(p):
        return pltpu.make_async_remote_copy(
            src_ref=bout.at[p], dst_ref=bin_.at[p],
            send_sem=bsend.at[p], recv_sem=brecv.at[p],
            device_id=(g - 1, col), device_id_type=MESH,
        )

    order = sorted(range(1, nz), key=lambda d: abs(2 * d - nz)) + [0]

    def chunk(dx, dz):
        rows = per * size
        at = pl.ds(pl.multiple_of(place(dx, dz) * rows, rows), rows)
        both = times_transposed(operand[...], high_ref[at, :])
        return both[:wide] + both[wide:] + times_transposed(operand[:wide, :], low_ref[at, :])

    def first(p):
        @pl.when(g > 0)
        def _():
            for dz in range(nz):
                z_copy(p, dz).wait_recv()
            total = zin[p, 0]
            for dz in range(1, nz):
                total = total + zin[p, dz]
            bout[p] = total
            back(p).start()

        span = pl.ds(pl.multiple_of(p * wide, wide), wide)
        for t in range(per):
            right, rest = split(src_ref[t, span, :] - bout[p, t])
            both = times_transposed(jnp.concatenate([right, rest], axis=0), inv_high[t])
            current = both[:wide] + both[wide:] + times_transposed(right, inv_low[t])
            solved_ref[t, span, :] = current
            high, low = split(current)
            operand[:wide, t * size:(t + 1) * size] = high
            operand[wide:, t * size:(t + 1) * size] = low

        for dz in order:
            for dx in range(1, nx):
                result = chunk(dx, dz)
                for t in range(per):
                    xout[p, dx - 1, dz, t] = result[:, t * size:(t + 1) * size]
                x_copy(p, dx, dz).start()
        for dz in order:
            result = chunk(0, dz)
            for t in range(per):
                own[p, dz, t] = result[:, t * size:(t + 1) * size]

    def second(p):
        for dz in order:
            for dx in range(1, nx):
                x_copy(p, dx, dz).wait_recv()
            part = own[p, dz]
            for dx in range(1, nx):
                part = part + xin[p, dx - 1, dz]
            zout[p, dz] = part

            @pl.when(inner)
            def _():
                z_copy(p, dz).start()

            if dz > 0:
                @pl.when(last)
                def _():
                    last_copy(p, dz).start()

    def tick(moment, carry):
        @pl.when(moment < panels)
        def _():
            first(moment)

        @pl.when(moment > 0)
        def _():
            second(moment - 1)

        return carry

    lax.fori_loop(0, panels + 1, tick, 0)

    def close(p, carry):
        span = pl.ds(pl.multiple_of(p * wide, wide), wide)

        @pl.when(last)
        def _():
            total = zout[p, 0]
            for dz in range(1, nz):
                last_copy(p, dz).wait_recv()
                total = total + zlast[p, dz]
            leaving_ref[:, span, :] = total
            for dz in range(1, nz):
                last_copy(p, dz).wait_send()

        @pl.when(inner)
        def _():
            back(p).wait_recv()
            leaving_ref[:, span, :] = bin_[p]
            for dz in range(nz):
                z_copy(p, dz).wait_send()

        for dz in order:
            for dx in range(1, nx):
                x_copy(p, dx, dz).wait_send()

        @pl.when(g > 0)
        def _():
            back(p).wait_send()

        return carry

    lax.fori_loop(0, panels, close, 0)


def local(nx, groups, col_devices, sources, diag_inverse, factor_tiles, tile_rows, tile_cols):
    per, panel_sources, size = sources.shape[1:]
    nz = col_devices // nx
    panels = PANELS if panel_sources % (16 * PANELS) == 0 else 1
    high, low = merge(factor_tiles[0], tile_rows, tile_cols, per * col_devices, per)
    block = (per, panel_sources, size)
    cut = (per, panel_sources // panels, size)
    whole = pl.BlockSpec(memory_space=pltpu.VMEM)
    dma = pltpu.SemaphoreType.DMA
    by_x = (panels, nx - 1, nz)
    by_z = (panels, nz)
    solved, leaving = pl.pallas_call(
        functools.partial(chain_kernel, groups, nx, nz, panels),
        out_shape=[jax.ShapeDtypeStruct(block, jnp.float32)] * 2,
        in_specs=[whole] * 4,
        out_specs=[whole] * 2,
        scratch_shapes=[
            pltpu.VMEM((per, size, size), jnp.bfloat16),
            pltpu.VMEM((per, size, size), jnp.bfloat16),
            pltpu.VMEM((2 * cut[1], per * size), jnp.bfloat16),
            pltpu.VMEM(by_z + cut, jnp.float32),
            pltpu.VMEM(by_x + cut, jnp.float32),
            pltpu.VMEM(by_x + cut, jnp.float32),
            pltpu.VMEM(by_z + cut, jnp.float32),
            pltpu.VMEM(by_z + cut, jnp.float32),
            pltpu.VMEM(by_z + cut, jnp.float32),
            pltpu.VMEM((panels,) + cut, jnp.float32),
            pltpu.VMEM((panels,) + cut, jnp.float32),
            dma(by_x),
            dma(by_x),
            dma(by_z),
            dma(by_z),
            dma(by_z),
            dma((panels,)),
            dma((panels,)),
        ],
        compiler_params=pltpu.CompilerParams(
            collective_id=0, has_side_effects=True, vmem_limit_bytes=36 * MIB
        ),
    )(sources[0], diag_inverse[0], high, low)
    return (solved[None], leaving[None])


def solution(mesh):
    groups, col_devices = mesh.shape["chain"], mesh.shape["col"]
    nx = max(d for d in range(1, col_devices + 1) if col_devices % d == 0 and d * d <= col_devices)
    return jax.shard_map(
        functools.partial(local, nx, groups, col_devices),
        mesh=mesh,
        in_specs=(
            P("chain", "col", None, None),
            P("chain", "col", None, None),
            P("chain", "col", None, None),
            P("chain", "col"),
            P("chain", "col"),
        ),
        out_specs=(P("chain", "col", None, None), P("chain", "col", None, None)),
        check_vma=False,
    )
```

```python
import functools

import jax
import jax.numpy as jnp
from jax import lax
from jax.experimental import pallas as pl
from jax.experimental.pallas import tpu as pltpu
from jax.sharding import PartitionSpec as P

MESH = pl.DeviceIdType.MESH
MIB = 1 << 20
PANELS = 2


def split(value):
    high = value.astype(jnp.bfloat16)
    low = (value - high.astype(jnp.float32)).astype(jnp.bfloat16)
    return high, low


def times_transposed(left, right):
    return lax.dot_general(left, right, (((1,), (1,)), ((), ())), preferred_element_type=jnp.float32)


def merge_kernel(pieces, rows_ref, cols_ref, factor_ref, high_ref, low_ref, held, total, arrived):
    tiles, size, _ = factor_ref.shape
    width = high_ref.shape[1] // size
    blocks = high_ref.shape[0] // size

    def fetch(i):
        span = pl.ds(pieces[i], pieces[i + 1] - pieces[i])
        return pltpu.make_async_copy(factor_ref.at[span], held.at[span], arrived.at[i])

    for i in range(len(pieces) - 1):
        fetch(i).start()

    def clear(block, carry):
        at = pl.ds(pl.multiple_of(block * size, size), size)
        total[at, :] = jnp.zeros((size, total.shape[1]), jnp.float32)
        return carry

    lax.fori_loop(0, blocks, clear, 0)

    def add(k, carry):
        row = pl.ds(pl.multiple_of(rows_ref[0, k] * size, size), size)
        col = pl.ds(pl.multiple_of(lax.rem(cols_ref[0, k], width) * size, size), size)
        total[row, col] += held[k]
        return carry

    for i in range(len(pieces) - 1):
        fetch(i).wait()
        lax.fori_loop(pieces[i], pieces[i + 1], add, 0)

    def finish(block, carry):
        at = pl.ds(pl.multiple_of(block * size, size), size)
        for c in range(width):
            cs = slice(c * size, (c + 1) * size)
            high, low = split(total[at, cs])
            high_ref[at, cs] = high
            low_ref[at, cs] = low
        return carry

    lax.fori_loop(0, blocks, finish, 0)


def merge(factor, rows, cols, row_tiles, col_tiles):
    tiles, size, _ = factor.shape
    pieces = list(range(0, tiles, 16)) + [tiles]
    shape = (row_tiles * size, col_tiles * size)
    whole = pl.BlockSpec(memory_space=pltpu.VMEM)
    scalars = pl.BlockSpec(memory_space=pltpu.SMEM)
    return pl.pallas_call(
        functools.partial(merge_kernel, pieces),
        out_shape=[pltpu.VMEM(shape, jnp.bfloat16)] * 2,
        in_specs=[scalars, scalars, pl.BlockSpec(memory_space=pltpu.HBM)],
        out_specs=[whole] * 2,
        scratch_shapes=[
            pltpu.VMEM(factor.shape, jnp.float32),
            pltpu.VMEM(shape, jnp.float32),
            pltpu.SemaphoreType.DMA((len(pieces) - 1,)),
        ],
        compiler_params=pltpu.CompilerParams(vmem_limit_bytes=40 * MIB),
    )(*(pltpu.with_memory_space_constraint(a, pltpu.HBM) for a in (rows, cols, factor)))


def chain_kernel(
    groups, nx, nz, panels,
    src_ref, inv_ref, high_ref, low_ref, solved_ref, leaving_ref,
    inv_high, inv_low, operand, own, xout, xin, zout, zin, zlast, bout, bin_,
    xsend, xrecv, zsend, zrecv, lrecv, bsend, brecv,
):
    g = lax.axis_index("chain")
    col = lax.axis_index("col")
    x = lax.rem(col, nx)
    z = lax.div(col, nx)
    per, sources, size = src_ref.shape
    wide = sources // panels
    last = g == groups - 1
    inner = jnp.logical_not(last)

    def place(dx, dz):
        return lax.rem(z + dz, nz) * nx + lax.rem(x + dx, nx)

    barrier = pltpu.get_barrier_semaphore()

    def greet(chain, dx, dz):
        pl.semaphore_signal(barrier, inc=1, device_id=(chain, place(dx, dz)), device_id_type=MESH)

    for dx in range(1, nx):
        greet(g, dx, 0)

    @pl.when(g > 0)
    def _():
        for dz in range(nz):
            greet(g - 1, 0, dz)

    @pl.when(inner)
    def _():
        for dz in range(nz):
            greet(g + 1, 0, dz)

    @pl.when(last)
    def _():
        for dz in range(1, nz):
            greet(g, 0, dz)

    for t in range(per):
        inv_high[t], inv_low[t] = split(inv_ref[t])

    @pl.when(g == 0)
    def _():
        bout[...] = jnp.zeros(bout.shape, jnp.float32)

    awaited = (nx - 1) + jnp.where(g > 0, nz, 0) + jnp.where(last, nz - 1, nz)
    pl.semaphore_wait(barrier, awaited)

    def x_copy(p, dx, dz):
        return pltpu.make_async_remote_copy(
            src_ref=xout.at[p, dx - 1, dz], dst_ref=xin.at[p, dx - 1, dz],
            send_sem=xsend.at[p, dx - 1, dz], recv_sem=xrecv.at[p, dx - 1, dz],
            device_id=(g, place(dx, 0)), device_id_type=MESH,
        )

    def z_copy(p, dz):
        return pltpu.make_async_remote_copy(
            src_ref=zout.at[p, dz], dst_ref=zin.at[p, dz],
            send_sem=zsend.at[p, dz], recv_sem=zrecv.at[p, dz],
            device_id=(g + 1, place(0, dz)), device_id_type=MESH,
        )

    def last_copy(p, dz):
        return pltpu.make_async_remote_copy(
            src_ref=zout.at[p, dz], dst_ref=zlast.at[p, dz],
            send_sem=zsend.at[p, dz], recv_sem=lrecv.at[p, dz],
            device_id=(g, place(0, dz)), device_id_type=MESH,
        )

    def back(p):
        return pltpu.make_async_remote_copy(
            src_ref=bout.at[p], dst_ref=bin_.at[p],
            send_sem=bsend.at[p], recv_sem=brecv.at[p],
            device_id=(g - 1, col), device_id_type=MESH,
        )

    order = sorted(range(1, nz), key=lambda d: abs(2 * d - nz)) + [0]

    def chunk(dx, dz):
        rows = per * size
        at = pl.ds(pl.multiple_of(place(dx, dz) * rows, rows), rows)
        both = times_transposed(operand[...], high_ref[at, :])
        return both[:wide] + both[wide:] + times_transposed(operand[:wide, :], low_ref[at, :])

    def first(p):
        @pl.when(g > 0)
        def _():
            for dz in range(nz):
                z_copy(p, dz).wait_recv()
            total = zin[p, 0]
            for dz in range(1, nz):
                total = total + zin[p, dz]
            bout[p] = total
            back(p).start()

        span = pl.ds(pl.multiple_of(p * wide, wide), wide)
        for t in range(per):
            right, rest = split(src_ref[t, span, :] - bout[p, t])
            both = times_transposed(jnp.concatenate([right, rest], axis=0), inv_high[t])
            current = both[:wide] + both[wide:] + times_transposed(right, inv_low[t])
            solved_ref[t, span, :] = current
            high, low = split(current)
            operand[:wide, t * size:(t + 1) * size] = high
            operand[wide:, t * size:(t + 1) * size] = low

        for dz in order:
            for dx in range(1, nx):
                result = chunk(dx, dz)
                for t in range(per):
                    xout[p, dx - 1, dz, t] = result[:, t * size:(t + 1) * size]
                x_copy(p, dx, dz).start()
        for dz in order:
            result = chunk(0, dz)
            for t in range(per):
                own[p, dz, t] = result[:, t * size:(t + 1) * size]

    def second(p):
        for dz in order:
            for dx in range(1, nx):
                x_copy(p, dx, dz).wait_recv()
            part = own[p, dz]
            for dx in range(1, nx):
                part = part + xin[p, dx - 1, dz]
            zout[p, dz] = part

            @pl.when(inner)
            def _():
                z_copy(p, dz).start()

            if dz > 0:
                @pl.when(last)
                def _():
                    last_copy(p, dz).start()

    def tick(p, carry):
        first(p)
        second(p)
        return carry

    lax.fori_loop(0, panels, tick, 0)

    def close(p, carry):
        span = pl.ds(pl.multiple_of(p * wide, wide), wide)

        @pl.when(last)
        def _():
            total = zout[p, 0]
            for dz in range(1, nz):
                last_copy(p, dz).wait_recv()
                total = total + zlast[p, dz]
            leaving_ref[:, span, :] = total
            for dz in range(1, nz):
                last_copy(p, dz).wait_send()

        @pl.when(inner)
        def _():
            back(p).wait_recv()
            leaving_ref[:, span, :] = bin_[p]
            for dz in range(nz):
                z_copy(p, dz).wait_send()

        for dz in order:
            for dx in range(1, nx):
                x_copy(p, dx, dz).wait_send()

        @pl.when(g > 0)
        def _():
            back(p).wait_send()

        return carry

    lax.fori_loop(0, panels, close, 0)


def local(nx, groups, col_devices, sources, diag_inverse, factor_tiles, tile_rows, tile_cols):
    per, panel_sources, size = sources.shape[1:]
    nz = col_devices // nx
    panels = PANELS if panel_sources % (16 * PANELS) == 0 else 1
    high, low = merge(factor_tiles[0], tile_rows, tile_cols, per * col_devices, per)
    block = (per, panel_sources, size)
    cut = (per, panel_sources // panels, size)
    whole = pl.BlockSpec(memory_space=pltpu.VMEM)
    dma = pltpu.SemaphoreType.DMA
    by_x = (panels, nx - 1, nz)
    by_z = (panels, nz)
    solved, leaving = pl.pallas_call(
        functools.partial(chain_kernel, groups, nx, nz, panels),
        out_shape=[jax.ShapeDtypeStruct(block, jnp.float32)] * 2,
        in_specs=[whole] * 4,
        out_specs=[whole] * 2,
        scratch_shapes=[
            pltpu.VMEM((per, size, size), jnp.bfloat16),
            pltpu.VMEM((per, size, size), jnp.bfloat16),
            pltpu.VMEM((2 * cut[1], per * size), jnp.bfloat16),
            pltpu.VMEM(by_z + cut, jnp.float32),
            pltpu.VMEM(by_x + cut, jnp.float32),
            pltpu.VMEM(by_x + cut, jnp.float32),
            pltpu.VMEM(by_z + cut, jnp.float32),
            pltpu.VMEM(by_z + cut, jnp.float32),
            pltpu.VMEM(by_z + cut, jnp.float32),
            pltpu.VMEM((panels,) + cut, jnp.float32),
            pltpu.VMEM((panels,) + cut, jnp.float32),
            dma(by_x),
            dma(by_x),
            dma(by_z),
            dma(by_z),
            dma(by_z),
            dma((panels,)),
            dma((panels,)),
        ],
        compiler_params=pltpu.CompilerParams(
            collective_id=0, has_side_effects=True, vmem_limit_bytes=36 * MIB
        ),
    )(sources[0], diag_inverse[0], high, low)
    return (solved[None], leaving[None])


def solution(mesh):
    groups, col_devices = mesh.shape["chain"], mesh.shape["col"]
    nx = max(d for d in range(1, col_devices + 1) if col_devices % d == 0 and d * d <= col_devices)
    return jax.shard_map(
        functools.partial(local, nx, groups, col_devices),
        mesh=mesh,
        in_specs=(
            P("chain", "col", None, None),
            P("chain", "col", None, None),
            P("chain", "col", None, None),
            P("chain", "col"),
            P("chain", "col"),
        ),
        out_specs=(P("chain", "col", None, None), P("chain", "col", None, None)),
        check_vma=False,
    )
```

```python
import functools

import jax
import jax.numpy as jnp
from jax import lax
from jax.experimental import pallas as pl
from jax.experimental.pallas import tpu as pltpu
from jax.sharding import PartitionSpec as P

MESH = pl.DeviceIdType.MESH
MIB = 1 << 20
PANELS = 2


def split(value):
    high = value.astype(jnp.bfloat16)
    low = (value - high.astype(jnp.float32)).astype(jnp.bfloat16)
    return high, low


def times_transposed(left, right):
    return lax.dot_general(left, right, (((1,), (1,)), ((), ())), preferred_element_type=jnp.float32)


def times(left, right):
    return lax.dot_general(left, right, (((1,), (0,)), ((), ())), preferred_element_type=jnp.float32)


def merge_kernel(pieces, rows_ref, cols_ref, factor_ref, high_ref, low_ref, held, total, named, arrived):
    tiles, size, _ = factor_ref.shape
    chunks = high_ref.shape[0]
    width = high_ref.shape[1] // size

    def fetch(i):
        span = pl.ds(pieces[i], pieces[i + 1] - pieces[i])
        return pltpu.make_async_copy(factor_ref.at[span], held.at[span], arrived.at[i])

    for i in range(len(pieces) - 1):
        fetch(i).start()

    def clear(place, carry):
        named[place] = 0
        return carry

    lax.fori_loop(0, chunks * width * width, clear, 0)

    def add(k, carry):
        place = rows_ref[0, k] * width + lax.rem(cols_ref[0, k], width)
        fresh = named[place] == 0
        named[place] = 1

        @pl.when(fresh)
        def _():
            total[place] = held[k]

        @pl.when(jnp.logical_not(fresh))
        def _():
            total[place] += held[k]

        return carry

    for i in range(len(pieces) - 1):
        fetch(i).wait()
        lax.fori_loop(pieces[i], pieces[i + 1], add, 0)

    def finish(chunk, carry):
        for r in range(width):
            for c in range(width):
                place = (chunk * width + r) * width + c
                cs, rs = slice(c * size, (c + 1) * size), slice(r * size, (r + 1) * size)

                @pl.when(named[place] != 0)
                def _():
                    high, low = split(total[place].T)
                    high_ref[chunk, cs, rs] = high
                    low_ref[chunk, cs, rs] = low

                @pl.when(named[place] == 0)
                def _():
                    high_ref[chunk, cs, rs] = jnp.zeros((size, size), jnp.bfloat16)
                    low_ref[chunk, cs, rs] = jnp.zeros((size, size), jnp.bfloat16)

        return carry

    lax.fori_loop(0, chunks, finish, 0)


def merge(factor, rows, cols, chunks, width):
    tiles, size, _ = factor.shape
    pieces = list(range(0, tiles, 16)) + [tiles]
    shape = (chunks, width * size, width * size)
    whole = pl.BlockSpec(memory_space=pltpu.VMEM)
    scalars = pl.BlockSpec(memory_space=pltpu.SMEM)
    return pl.pallas_call(
        functools.partial(merge_kernel, pieces),
        out_shape=[pltpu.VMEM(shape, jnp.bfloat16)] * 2,
        in_specs=[scalars, scalars, pl.BlockSpec(memory_space=pltpu.HBM)],
        out_specs=[whole] * 2,
        scratch_shapes=[
            pltpu.VMEM(factor.shape, jnp.float32),
            pltpu.VMEM((chunks * width * width, size, size), jnp.float32),
            pltpu.SMEM((chunks * width * width,), jnp.int32),
            pltpu.SemaphoreType.DMA((len(pieces) - 1,)),
        ],
        compiler_params=pltpu.CompilerParams(vmem_limit_bytes=40 * MIB),
    )(*(pltpu.with_memory_space_constraint(a, pltpu.HBM) for a in (rows, cols, factor)))


def chain_kernel(
    groups, nx, nz, panels,
    src_ref, inv_ref, high_ref, low_ref, solved_ref, leaving_ref,
    inv_high, inv_low, operand, own, xout, xin, zout, zin, zlast, bout, bin_,
    xsend, xrecv, zsend, zrecv, lrecv, bsend, brecv,
):
    g = lax.axis_index("chain")
    col = lax.axis_index("col")
    x = lax.rem(col, nx)
    z = lax.div(col, nx)
    per, sources, size = src_ref.shape
    wide = sources // panels
    last = g == groups - 1
    inner = jnp.logical_not(last)

    def place(dx, dz):
        return lax.rem(z + dz, nz) * nx + lax.rem(x + dx, nx)

    barrier = pltpu.get_barrier_semaphore()

    def greet(chain, dx, dz):
        pl.semaphore_signal(barrier, inc=1, device_id=(chain, place(dx, dz)), device_id_type=MESH)

    for dx in range(1, nx):
        greet(g, dx, 0)

    @pl.when(g > 0)
    def _():
        for dz in range(nz):
            greet(g - 1, 0, dz)

    @pl.when(inner)
    def _():
        for dz in range(nz):
            greet(g + 1, 0, dz)

    @pl.when(last)
    def _():
        for dz in range(1, nz):
            greet(g, 0, dz)

    for t in range(per):
        inv_high[t], inv_low[t] = split(inv_ref[t])

    @pl.when(g == 0)
    def _():
        bout[...] = jnp.zeros(bout.shape, jnp.float32)

    awaited = (nx - 1) + jnp.where(g > 0, nz, 0) + jnp.where(last, nz - 1, nz)
    pl.semaphore_wait(barrier, awaited)

    def x_copy(p, dx, dz):
        return pltpu.make_async_remote_copy(
            src_ref=xout.at[p, dx - 1, dz], dst_ref=xin.at[p, dx - 1, dz],
            send_sem=xsend.at[p, dx - 1, dz], recv_sem=xrecv.at[p, dx - 1, dz],
            device_id=(g, place(dx, 0)), device_id_type=MESH,
        )

    def z_copy(p, dz):
        return pltpu.make_async_remote_copy(
            src_ref=zout.at[p, dz], dst_ref=zin.at[p, dz],
            send_sem=zsend.at[p, dz], recv_sem=zrecv.at[p, dz],
            device_id=(g + 1, place(0, dz)), device_id_type=MESH,
        )

    def last_copy(p, dz):
        return pltpu.make_async_remote_copy(
            src_ref=zout.at[p, dz], dst_ref=zlast.at[p, dz],
            send_sem=zsend.at[p, dz], recv_sem=lrecv.at[p, dz],
            device_id=(g, place(0, dz)), device_id_type=MESH,
        )

    def back(p):
        return pltpu.make_async_remote_copy(
            src_ref=bout.at[p], dst_ref=bin_.at[p],
            send_sem=bsend.at[p], recv_sem=brecv.at[p],
            device_id=(g - 1, col), device_id_type=MESH,
        )

    order = sorted(range(1, nz), key=lambda d: abs(2 * d - nz)) + [0]

    def chunk(dx, dz):
        at = place(dx, dz)
        both = times(operand[...], high_ref[at])
        return both[:wide] + both[wide:] + times(operand[:wide, :], low_ref[at])

    def first(p):
        @pl.when(g > 0)
        def _():
            for dz in range(nz):
                z_copy(p, dz).wait_recv()
            total = zin[p, 0]
            for dz in range(1, nz):
                total = total + zin[p, dz]
            bout[p] = total
            back(p).start()

        span = pl.ds(pl.multiple_of(p * wide, wide), wide)
        for t in range(per):
            right, rest = split(src_ref[t, span, :] - bout[p, t])
            both = times_transposed(jnp.concatenate([right, rest], axis=0), inv_high[t])
            current = both[:wide] + both[wide:] + times_transposed(right, inv_low[t])
            solved_ref[t, span, :] = current
            high, low = split(current)
            operand[:wide, t * size:(t + 1) * size] = high
            operand[wide:, t * size:(t + 1) * size] = low

        for dz in order:
            for dx in range(1, nx):
                result = chunk(dx, dz)
                for t in range(per):
                    xout[p, dx - 1, dz, t] = result[:, t * size:(t + 1) * size]
                x_copy(p, dx, dz).start()
        for dz in order:
            result = chunk(0, dz)
            for t in range(per):
                own[p, dz, t] = result[:, t * size:(t + 1) * size]

    def second(p):
        for dz in order:
            for dx in range(1, nx):
                x_copy(p, dx, dz).wait_recv()
            part = own[p, dz]
            for dx in range(1, nx):
                part = part + xin[p, dx - 1, dz]
            zout[p, dz] = part

            @pl.when(inner)
            def _():
                z_copy(p, dz).start()

            if dz > 0:
                @pl.when(last)
                def _():
                    last_copy(p, dz).start()

    def tick(p, carry):
        first(p)
        second(p)
        return carry

    lax.fori_loop(0, panels, tick, 0)

    def close(p, carry):
        span = pl.ds(pl.multiple_of(p * wide, wide), wide)

        @pl.when(last)
        def _():
            total = zout[p, 0]
            for dz in range(1, nz):
                last_copy(p, dz).wait_recv()
                total = total + zlast[p, dz]
            leaving_ref[:, span, :] = total
            for dz in range(1, nz):
                last_copy(p, dz).wait_send()

        @pl.when(inner)
        def _():
            back(p).wait_recv()
            leaving_ref[:, span, :] = bin_[p]
            for dz in range(nz):
                z_copy(p, dz).wait_send()

        for dz in order:
            for dx in range(1, nx):
                x_copy(p, dx, dz).wait_send()

        @pl.when(g > 0)
        def _():
            back(p).wait_send()

        return carry

    lax.fori_loop(0, panels, close, 0)


def local(nx, groups, col_devices, sources, diag_inverse, factor_tiles, tile_rows, tile_cols):
    per, panel_sources, size = sources.shape[1:]
    nz = col_devices // nx
    panels = PANELS if panel_sources % (16 * PANELS) == 0 else 1
    high, low = merge(factor_tiles[0], tile_rows, tile_cols, col_devices, per)
    block = (per, panel_sources, size)
    cut = (per, panel_sources // panels, size)
    whole = pl.BlockSpec(memory_space=pltpu.VMEM)
    dma = pltpu.SemaphoreType.DMA
    by_x = (panels, nx - 1, nz)
    by_z = (panels, nz)
    solved, leaving = pl.pallas_call(
        functools.partial(chain_kernel, groups, nx, nz, panels),
        out_shape=[jax.ShapeDtypeStruct(block, jnp.float32)] * 2,
        in_specs=[whole] * 4,
        out_specs=[whole] * 2,
        scratch_shapes=[
            pltpu.VMEM((per, size, size), jnp.bfloat16),
            pltpu.VMEM((per, size, size), jnp.bfloat16),
            pltpu.VMEM((2 * cut[1], per * size), jnp.bfloat16),
            pltpu.VMEM(by_z + cut, jnp.float32),
            pltpu.VMEM(by_x + cut, jnp.float32),
            pltpu.VMEM(by_x + cut, jnp.float32),
            pltpu.VMEM(by_z + cut, jnp.float32),
            pltpu.VMEM(by_z + cut, jnp.float32),
            pltpu.VMEM(by_z + cut, jnp.float32),
            pltpu.VMEM((panels,) + cut, jnp.float32),
            pltpu.VMEM((panels,) + cut, jnp.float32),
            dma(by_x),
            dma(by_x),
            dma(by_z),
            dma(by_z),
            dma(by_z),
            dma((panels,)),
            dma((panels,)),
        ],
        compiler_params=pltpu.CompilerParams(
            collective_id=0, has_side_effects=True, vmem_limit_bytes=36 * MIB
        ),
    )(sources[0], diag_inverse[0], high, low)
    return (solved[None], leaving[None])


def solution(mesh):
    groups, col_devices = mesh.shape["chain"], mesh.shape["col"]
    nx = max(d for d in range(1, col_devices + 1) if col_devices % d == 0 and d * d <= col_devices)
    return jax.shard_map(
        functools.partial(local, nx, groups, col_devices),
        mesh=mesh,
        in_specs=(
            P("chain", "col", None, None),
            P("chain", "col", None, None),
            P("chain", "col", None, None),
            P("chain", "col"),
            P("chain", "col"),
        ),
        out_specs=(P("chain", "col", None, None), P("chain", "col", None, None)),
        check_vma=False,
    )
```

```python
import functools

import jax
import jax.numpy as jnp
from jax import lax
from jax.experimental import pallas as pl
from jax.experimental.pallas import tpu as pltpu
from jax.sharding import PartitionSpec as P

MESH = pl.DeviceIdType.MESH
MIB = 1 << 20
PANELS = 2


def split(value):
    high = value.astype(jnp.bfloat16)
    low = (value - high.astype(jnp.float32)).astype(jnp.bfloat16)
    return high, low


def times_transposed(left, right):
    return lax.dot_general(left, right, (((1,), (1,)), ((), ())), preferred_element_type=jnp.float32)


def merge_kernel(pieces, rows_ref, cols_ref, factor_ref, high_ref, low_ref, held, total, arrived):
    tiles, size, _ = factor_ref.shape
    width = high_ref.shape[1] // size
    blocks = high_ref.shape[0] // size

    def fetch(i):
        span = pl.ds(pieces[i], pieces[i + 1] - pieces[i])
        return pltpu.make_async_copy(factor_ref.at[span], held.at[span], arrived.at[i])

    for i in range(len(pieces) - 1):
        fetch(i).start()

    def clear(block, carry):
        at = pl.ds(pl.multiple_of(block * size, size), size)
        total[at, :] = jnp.zeros((size, total.shape[1]), jnp.float32)
        return carry

    lax.fori_loop(0, blocks, clear, 0)

    def add(k, carry):
        row = pl.ds(pl.multiple_of(rows_ref[0, k] * size, size), size)
        col = pl.ds(pl.multiple_of(lax.rem(cols_ref[0, k], width) * size, size), size)
        total[row, col] += held[k]
        return carry

    for i in range(len(pieces) - 1):
        fetch(i).wait()
        lax.fori_loop(pieces[i], pieces[i + 1], add, 0)

    def finish(block, carry):
        at = pl.ds(pl.multiple_of(block * size, size), size)
        for c in range(width):
            cs = slice(c * size, (c + 1) * size)
            high, low = split(total[at, cs])
            high_ref[at, cs] = high
            low_ref[at, cs] = low
        return carry

    lax.fori_loop(0, blocks, finish, 0)


def merge(factor, rows, cols, row_tiles, col_tiles):
    tiles, size, _ = factor.shape
    pieces = list(range(0, tiles, 16)) + [tiles]
    shape = (row_tiles * size, col_tiles * size)
    whole = pl.BlockSpec(memory_space=pltpu.VMEM)
    scalars = pl.BlockSpec(memory_space=pltpu.SMEM)
    return pl.pallas_call(
        functools.partial(merge_kernel, pieces),
        out_shape=[pltpu.VMEM(shape, jnp.bfloat16)] * 2,
        in_specs=[scalars, scalars, pl.BlockSpec(memory_space=pltpu.HBM)],
        out_specs=[whole] * 2,
        scratch_shapes=[
            pltpu.VMEM(factor.shape, jnp.float32),
            pltpu.VMEM(shape, jnp.float32),
            pltpu.SemaphoreType.DMA((len(pieces) - 1,)),
        ],
        compiler_params=pltpu.CompilerParams(vmem_limit_bytes=40 * MIB),
    )(*(pltpu.with_memory_space_constraint(a, pltpu.HBM) for a in (rows, cols, factor)))


def chain_kernel(
    groups, nx, nz, panels,
    src_ref, inv_ref, high_ref, low_ref, solved_ref, leaving_ref,
    inv_high, inv_low, operand, xout, xin, zout, zin, zlast, bout, bin_, whole, fed_in,
    xsend, xrecv, zsend, zrecv, lrecv, bsend, brecv, fsend, frecv,
):
    g = lax.axis_index("chain")
    col = lax.axis_index("col")
    x = lax.rem(col, nx)
    z = lax.div(col, nx)
    per, sources, size = src_ref.shape
    wide = sources // panels
    last = g == groups - 1
    odd = lax.rem(g, 2) == 1
    even = jnp.logical_not(odd)
    keeps = odd | last
    near = jnp.logical_not(keeps)
    far = odd & jnp.logical_not(last)
    fed = even & (g > 0)

    def place(dx, dz):
        return lax.rem(z + dz, nz) * nx + lax.rem(x + dx, nx)

    barrier = pltpu.get_barrier_semaphore()

    def greet(chain, dx, dz):
        pl.semaphore_signal(barrier, inc=1, device_id=(chain, place(dx, dz)), device_id_type=MESH)

    for dx in range(1, nx):
        greet(g, dx, 0)

    @pl.when(odd)
    def _():
        for dz in range(nz):
            greet(g - 1, 0, dz)

    @pl.when(near)
    def _():
        for dz in range(nz):
            greet(g + 1, 0, dz)

    @pl.when(keeps)
    def _():
        for dz in range(1, nz):
            greet(g, 0, dz)

    @pl.when(far)
    def _():
        greet(g + 1, 0, 0)

    @pl.when(fed)
    def _():
        greet(g - 1, 0, 0)

    for t in range(per):
        inv_high[t], inv_low[t] = split(inv_ref[t])

    @pl.when(g == 0)
    def _():
        bout[...] = jnp.zeros(bout.shape, jnp.float32)

    awaited = (
        (nx - 1) + jnp.where(odd, nz, 0) + jnp.where(keeps, nz - 1, nz)
        + jnp.where(far, 1, 0) + jnp.where(fed, 1, 0)
    )
    pl.semaphore_wait(barrier, awaited)

    def x_copy(p, dx, dz):
        return pltpu.make_async_remote_copy(
            src_ref=xout.at[p, dx - 1, dz], dst_ref=xin.at[p, dx - 1, dz],
            send_sem=xsend.at[p, dx - 1, dz], recv_sem=xrecv.at[p, dx - 1, dz],
            device_id=(g, place(dx, 0)), device_id_type=MESH,
        )

    def z_copy(p, dz):
        return pltpu.make_async_remote_copy(
            src_ref=zout.at[p, dz], dst_ref=zin.at[p, dz],
            send_sem=zsend.at[p, dz], recv_sem=zrecv.at[p, dz],
            device_id=(g + 1, place(0, dz)), device_id_type=MESH,
        )

    def last_copy(p, dz):
        return pltpu.make_async_remote_copy(
            src_ref=zout.at[p, dz], dst_ref=zlast.at[p, dz],
            send_sem=zsend.at[p, dz], recv_sem=lrecv.at[p, dz],
            device_id=(g, place(0, dz)), device_id_type=MESH,
        )

    def back(p):
        return pltpu.make_async_remote_copy(
            src_ref=bout.at[p], dst_ref=bin_.at[p],
            send_sem=bsend.at[p], recv_sem=brecv.at[p],
            device_id=(g - 1, col), device_id_type=MESH,
        )

    def forward(p):
        return pltpu.make_async_remote_copy(
            src_ref=whole.at[p], dst_ref=fed_in.at[p],
            send_sem=fsend.at[p], recv_sem=frecv.at[p],
            device_id=(g + 1, col), device_id_type=MESH,
        )

    order = sorted(range(1, nz), key=lambda d: abs(2 * d - nz)) + [0]

    def chunk(dx, dz):
        rows = per * size
        at = pl.ds(pl.multiple_of(place(dx, dz) * rows, rows), rows)
        both = times_transposed(operand[...], high_ref[at, :])
        return both[:wide] + both[wide:] + times_transposed(operand[:wide, :], low_ref[at, :])

    def first(p):
        @pl.when(odd)
        def _():
            for dz in range(nz):
                z_copy(p, dz).wait_recv()
            total = zin[p, 0]
            for dz in range(1, nz):
                total = total + zin[p, dz]
            bout[p] = total
            back(p).start()

        @pl.when(fed)
        def _():
            forward(p).wait_recv()
            bout[p] = fed_in[p]

        span = pl.ds(pl.multiple_of(p * wide, wide), wide)
        for t in range(per):
            right, rest = split(src_ref[t, span, :] - bout[p, t])
            both = times_transposed(jnp.concatenate([right, rest], axis=0), inv_high[t])
            current = both[:wide] + both[wide:] + times_transposed(right, inv_low[t])
            solved_ref[t, span, :] = current
            high, low = split(current)
            operand[:wide, t * size:(t + 1) * size] = high
            operand[wide:, t * size:(t + 1) * size] = low

        for dz in order:
            for dx in range(1, nx):
                result = chunk(dx, dz)
                for t in range(per):
                    xout[p, dx - 1, dz, t] = result[:, t * size:(t + 1) * size]
                x_copy(p, dx, dz).start()

    def second(p):
        for dz in order:
            result = chunk(0, dz)
            for dx in range(1, nx):
                x_copy(p, dx, dz).wait_recv()
            for t in range(per):
                part = result[:, t * size:(t + 1) * size]
                for dx in range(1, nx):
                    part = part + xin[p, dx - 1, dz, t]
                zout[p, dz, t] = part

            @pl.when(near)
            def _():
                z_copy(p, dz).start()

            if dz > 0:
                @pl.when(keeps)
                def _():
                    last_copy(p, dz).start()

    def gather(p):
        total = zout[p, 0]
        for dz in range(1, nz):
            last_copy(p, dz).wait_recv()
            total = total + zlast[p, dz]
        whole[p] = total

    def tick(p, carry):
        first(p)
        second(p)

        @pl.when(far)
        def _():
            gather(p)
            forward(p).start()

        return carry

    lax.fori_loop(0, panels, tick, 0)

    def close(p, carry):
        span = pl.ds(pl.multiple_of(p * wide, wide), wide)

        @pl.when(last)
        def _():
            gather(p)

        @pl.when(keeps)
        def _():
            leaving_ref[:, span, :] = whole[p]
            for dz in range(1, nz):
                last_copy(p, dz).wait_send()

        @pl.when(far)
        def _():
            forward(p).wait_send()

        @pl.when(near)
        def _():
            back(p).wait_recv()
            leaving_ref[:, span, :] = bin_[p]
            for dz in range(nz):
                z_copy(p, dz).wait_send()

        for dz in order:
            for dx in range(1, nx):
                x_copy(p, dx, dz).wait_send()

        @pl.when(odd)
        def _():
            back(p).wait_send()

        return carry

    lax.fori_loop(0, panels, close, 0)


def local(nx, groups, col_devices, sources, diag_inverse, factor_tiles, tile_rows, tile_cols):
    per, panel_sources, size = sources.shape[1:]
    nz = col_devices // nx
    panels = PANELS if panel_sources % (16 * PANELS) == 0 else 1
    high, low = merge(factor_tiles[0], tile_rows, tile_cols, per * col_devices, per)
    block = (per, panel_sources, size)
    cut = (per, panel_sources // panels, size)
    whole = pl.BlockSpec(memory_space=pltpu.VMEM)
    dma = pltpu.SemaphoreType.DMA
    by_x = (panels, nx - 1, nz)
    by_z = (panels, nz)
    solved, leaving = pl.pallas_call(
        functools.partial(chain_kernel, groups, nx, nz, panels),
        out_shape=[jax.ShapeDtypeStruct(block, jnp.float32)] * 2,
        in_specs=[whole] * 4,
        out_specs=[whole] * 2,
        scratch_shapes=[
            pltpu.VMEM((per, size, size), jnp.bfloat16),
            pltpu.VMEM((per, size, size), jnp.bfloat16),
            pltpu.VMEM((2 * cut[1], per * size), jnp.bfloat16),
            pltpu.VMEM(by_x + cut, jnp.float32),
            pltpu.VMEM(by_x + cut, jnp.float32),
            pltpu.VMEM(by_z + cut, jnp.float32),
            pltpu.VMEM(by_z + cut, jnp.float32),
            pltpu.VMEM(by_z + cut, jnp.float32),
            pltpu.VMEM((panels,) + cut, jnp.float32),
            pltpu.VMEM((panels,) + cut, jnp.float32),
            pltpu.VMEM((panels,) + cut, jnp.float32),
            pltpu.VMEM((panels,) + cut, jnp.float32),
            dma(by_x),
            dma(by_x),
            dma(by_z),
            dma(by_z),
            dma(by_z),
            dma((panels,)),
            dma((panels,)),
            dma((panels,)),
            dma((panels,)),
        ],
        compiler_params=pltpu.CompilerParams(
            collective_id=0, has_side_effects=True, vmem_limit_bytes=36 * MIB
        ),
    )(sources[0], diag_inverse[0], high, low)
    return (solved[None], leaving[None])


def solution(mesh):
    groups, col_devices = mesh.shape["chain"], mesh.shape["col"]
    nx = max(d for d in range(1, col_devices + 1) if col_devices % d == 0 and d * d <= col_devices)
    return jax.shard_map(
        functools.partial(local, nx, groups, col_devices),
        mesh=mesh,
        in_specs=(
            P("chain", "col", None, None),
            P("chain", "col", None, None),
            P("chain", "col", None, None),
            P("chain", "col"),
            P("chain", "col"),
        ),
        out_specs=(P("chain", "col", None, None), P("chain", "col", None, None)),
        check_vma=False,
    )
```

```python
import functools

import jax
import jax.numpy as jnp
from jax import lax
from jax.experimental import pallas as pl
from jax.experimental.pallas import tpu as pltpu
from jax.sharding import PartitionSpec as P

MESH = pl.DeviceIdType.MESH
MIB = 1 << 20
PANELS = 2


def split(value):
    high = value.astype(jnp.bfloat16)
    low = (value - high.astype(jnp.float32)).astype(jnp.bfloat16)
    return high, low


def times_transposed(left, right):
    return lax.dot_general(left, right, (((1,), (1,)), ((), ())), preferred_element_type=jnp.float32)


def merge_kernel(pieces, rows_ref, cols_ref, factor_ref, high_ref, low_ref, held, total, arrived):
    tiles, size, _ = factor_ref.shape
    width = high_ref.shape[1] // size
    blocks = high_ref.shape[0] // size

    def fetch(i):
        span = pl.ds(pieces[i], pieces[i + 1] - pieces[i])
        return pltpu.make_async_copy(factor_ref.at[span], held.at[span], arrived.at[i])

    for i in range(len(pieces) - 1):
        fetch(i).start()

    def clear(block, carry):
        at = pl.ds(pl.multiple_of(block * size, size), size)
        total[at, :] = jnp.zeros((size, total.shape[1]), jnp.float32)
        return carry

    lax.fori_loop(0, blocks, clear, 0)

    def add(k, carry):
        row = pl.ds(pl.multiple_of(rows_ref[0, k] * size, size), size)
        col = pl.ds(pl.multiple_of(lax.rem(cols_ref[0, k], width) * size, size), size)
        total[row, col] += held[k]
        return carry

    for i in range(len(pieces) - 1):
        fetch(i).wait()
        lax.fori_loop(pieces[i], pieces[i + 1], add, 0)

    def finish(block, carry):
        at = pl.ds(pl.multiple_of(block * size, size), size)
        for c in range(width):
            cs = slice(c * size, (c + 1) * size)
            high, low = split(total[at, cs])
            high_ref[at, cs] = high
            low_ref[at, cs] = low
        return carry

    lax.fori_loop(0, blocks, finish, 0)


def merge(factor, rows, cols, row_tiles, col_tiles):
    tiles, size, _ = factor.shape
    pieces = list(range(0, tiles, 16)) + [tiles]
    shape = (row_tiles * size, col_tiles * size)
    whole = pl.BlockSpec(memory_space=pltpu.VMEM)
    scalars = pl.BlockSpec(memory_space=pltpu.SMEM)
    return pl.pallas_call(
        functools.partial(merge_kernel, pieces),
        out_shape=[pltpu.VMEM(shape, jnp.bfloat16)] * 2,
        in_specs=[scalars, scalars, pl.BlockSpec(memory_space=pltpu.HBM)],
        out_specs=[whole] * 2,
        scratch_shapes=[
            pltpu.VMEM(factor.shape, jnp.float32),
            pltpu.VMEM(shape, jnp.float32),
            pltpu.SemaphoreType.DMA((len(pieces) - 1,)),
        ],
        compiler_params=pltpu.CompilerParams(vmem_limit_bytes=40 * MIB),
    )(*(pltpu.with_memory_space_constraint(a, pltpu.HBM) for a in (rows, cols, factor)))


def chain_kernel(
    groups, nx, nz, panels,
    src_ref, inv_ref, high_ref, low_ref, solved_ref, leaving_ref,
    inv_high, inv_low, operand, own, xout, xin, zout, zin, zlast, bout, bin_, whole, fed_in,
    xsend, xrecv, zsend, zrecv, lrecv, bsend, brecv, fsend, frecv,
):
    g = lax.axis_index("chain")
    col = lax.axis_index("col")
    x = lax.rem(col, nx)
    z = lax.div(col, nx)
    per, sources, size = src_ref.shape
    wide = sources // panels
    last = g == groups - 1
    odd = lax.rem(g, 2) == 1
    even = jnp.logical_not(odd)
    keeps = odd | last
    near = jnp.logical_not(keeps)
    far = odd & jnp.logical_not(last)
    fed = even & (g > 0)

    def place(dx, dz):
        return lax.rem(z + dz, nz) * nx + lax.rem(x + dx, nx)

    barrier = pltpu.get_barrier_semaphore()

    def greet(chain, dx, dz):
        pl.semaphore_signal(barrier, inc=1, device_id=(chain, place(dx, dz)), device_id_type=MESH)

    for dx in range(1, nx):
        greet(g, dx, 0)

    @pl.when(odd)
    def _():
        for dz in range(nz):
            greet(g - 1, 0, dz)

    @pl.when(near)
    def _():
        for dz in range(nz):
            greet(g + 1, 0, dz)

    @pl.when(keeps)
    def _():
        for dz in range(1, nz):
            greet(g, 0, dz)

    @pl.when(far)
    def _():
        greet(g + 1, 0, 0)

    @pl.when(fed)
    def _():
        greet(g - 1, 0, 0)

    for t in range(per):
        inv_high[t], inv_low[t] = split(inv_ref[t])

    @pl.when(g == 0)
    def _():
        bout[...] = jnp.zeros(bout.shape, jnp.float32)

    awaited = (
        (nx - 1) + jnp.where(odd, nz, 0) + jnp.where(keeps, nz - 1, nz)
        + jnp.where(far, 1, 0) + jnp.where(fed, 1, 0)
    )
    pl.semaphore_wait(barrier, awaited)

    def x_copy(p, dx, dz):
        return pltpu.make_async_remote_copy(
            src_ref=xout.at[p, dx - 1, dz], dst_ref=xin.at[p, dx - 1, dz],
            send_sem=xsend.at[p, dx - 1, dz], recv_sem=xrecv.at[p, dx - 1, dz],
            device_id=(g, place(dx, 0)), device_id_type=MESH,
        )

    def z_copy(p, dz):
        return pltpu.make_async_remote_copy(
            src_ref=zout.at[p, dz], dst_ref=zin.at[p, dz],
            send_sem=zsend.at[p, dz], recv_sem=zrecv.at[p, dz],
            device_id=(g + 1, place(0, dz)), device_id_type=MESH,
        )

    def last_copy(p, dz):
        return pltpu.make_async_remote_copy(
            src_ref=zout.at[p, dz], dst_ref=zlast.at[p, dz],
            send_sem=zsend.at[p, dz], recv_sem=lrecv.at[p, dz],
            device_id=(g, place(0, dz)), device_id_type=MESH,
        )

    def back(p):
        return pltpu.make_async_remote_copy(
            src_ref=bout.at[p], dst_ref=bin_.at[p],
            send_sem=bsend.at[p], recv_sem=brecv.at[p],
            device_id=(g - 1, col), device_id_type=MESH,
        )

    def forward(p):
        return pltpu.make_async_remote_copy(
            src_ref=whole.at[p], dst_ref=fed_in.at[p],
            send_sem=fsend.at[p], recv_sem=frecv.at[p],
            device_id=(g + 1, col), device_id_type=MESH,
        )

    order = sorted(range(1, nz), key=lambda d: abs(2 * d - nz)) + [0]

    def chunk(dx, dz):
        rows = per * size
        at = pl.ds(pl.multiple_of(place(dx, dz) * rows, rows), rows)
        both = times_transposed(operand[...], high_ref[at, :])
        return both[:wide] + both[wide:] + times_transposed(operand[:wide, :], low_ref[at, :])

    def fill(dx, store):
        results = [chunk(dx, dz) for dz in order]
        for dz, result in zip(order, results):
            for t in range(per):
                store[dz, t] = result[:, t * size:(t + 1) * size]

    def first(p):
        @pl.when(odd)
        def _():
            for dz in range(nz):
                z_copy(p, dz).wait_recv()
            total = zin[p, 0]
            for dz in range(1, nz):
                total = total + zin[p, dz]
            bout[p] = total
            back(p).start()

        @pl.when(fed)
        def _():
            forward(p).wait_recv()
            bout[p] = fed_in[p]

        span = pl.ds(pl.multiple_of(p * wide, wide), wide)
        for t in range(per):
            right, rest = split(src_ref[t, span, :] - bout[p, t])
            both = times_transposed(jnp.concatenate([right, rest], axis=0), inv_high[t])
            current = both[:wide] + both[wide:] + times_transposed(right, inv_low[t])
            solved_ref[t, span, :] = current
            high, low = split(current)
            operand[:wide, t * size:(t + 1) * size] = high
            operand[wide:, t * size:(t + 1) * size] = low

        for dx in range(1, nx):
            fill(dx, xout.at[p, dx - 1])
            for dz in order:
                x_copy(p, dx, dz).start()
        fill(0, own.at[p])

    def second(p):
        for dz in order:
            for dx in range(1, nx):
                x_copy(p, dx, dz).wait_recv()
            part = own[p, dz]
            for dx in range(1, nx):
                part = part + xin[p, dx - 1, dz]
            zout[p, dz] = part

            @pl.when(near)
            def _():
                z_copy(p, dz).start()

            if dz > 0:
                @pl.when(keeps)
                def _():
                    last_copy(p, dz).start()

    def gather(p):
        total = zout[p, 0]
        for dz in range(1, nz):
            last_copy(p, dz).wait_recv()
            total = total + zlast[p, dz]
        whole[p] = total

    def tick(p, carry):
        first(p)
        second(p)

        @pl.when(far)
        def _():
            gather(p)
            forward(p).start()

        return carry

    lax.fori_loop(0, panels, tick, 0)

    def close(p, carry):
        span = pl.ds(pl.multiple_of(p * wide, wide), wide)

        @pl.when(last)
        def _():
            gather(p)

        @pl.when(keeps)
        def _():
            leaving_ref[:, span, :] = whole[p]
            for dz in range(1, nz):
                last_copy(p, dz).wait_send()

        @pl.when(far)
        def _():
            forward(p).wait_send()

        @pl.when(near)
        def _():
            back(p).wait_recv()
            leaving_ref[:, span, :] = bin_[p]
            for dz in range(nz):
                z_copy(p, dz).wait_send()

        for dz in order:
            for dx in range(1, nx):
                x_copy(p, dx, dz).wait_send()

        @pl.when(odd)
        def _():
            back(p).wait_send()

        return carry

    lax.fori_loop(0, panels, close, 0)


def local(nx, groups, col_devices, sources, diag_inverse, factor_tiles, tile_rows, tile_cols):
    per, panel_sources, size = sources.shape[1:]
    nz = col_devices // nx
    panels = PANELS if panel_sources % (16 * PANELS) == 0 else 1
    high, low = merge(factor_tiles[0], tile_rows, tile_cols, per * col_devices, per)
    block = (per, panel_sources, size)
    cut = (per, panel_sources // panels, size)
    whole = pl.BlockSpec(memory_space=pltpu.VMEM)
    dma = pltpu.SemaphoreType.DMA
    by_x = (panels, nx - 1, nz)
    by_z = (panels, nz)
    solved, leaving = pl.pallas_call(
        functools.partial(chain_kernel, groups, nx, nz, panels),
        out_shape=[jax.ShapeDtypeStruct(block, jnp.float32)] * 2,
        in_specs=[whole] * 4,
        out_specs=[whole] * 2,
        scratch_shapes=[
            pltpu.VMEM((per, size, size), jnp.bfloat16),
            pltpu.VMEM((per, size, size), jnp.bfloat16),
            pltpu.VMEM((2 * cut[1], per * size), jnp.bfloat16),
            pltpu.VMEM(by_z + cut, jnp.float32),
            pltpu.VMEM(by_x + cut, jnp.float32),
            pltpu.VMEM(by_x + cut, jnp.float32),
            pltpu.VMEM(by_z + cut, jnp.float32),
            pltpu.VMEM(by_z + cut, jnp.float32),
            pltpu.VMEM(by_z + cut, jnp.float32),
            pltpu.VMEM((panels,) + cut, jnp.float32),
            pltpu.VMEM((panels,) + cut, jnp.float32),
            pltpu.VMEM((panels,) + cut, jnp.float32),
            pltpu.VMEM((panels,) + cut, jnp.float32),
            dma(by_x),
            dma(by_x),
            dma(by_z),
            dma(by_z),
            dma(by_z),
            dma((panels,)),
            dma((panels,)),
            dma((panels,)),
            dma((panels,)),
        ],
        compiler_params=pltpu.CompilerParams(
            collective_id=0, has_side_effects=True, vmem_limit_bytes=36 * MIB
        ),
    )(sources[0], diag_inverse[0], high, low)
    return (solved[None], leaving[None])


def solution(mesh):
    groups, col_devices = mesh.shape["chain"], mesh.shape["col"]
    nx = max(d for d in range(1, col_devices + 1) if col_devices % d == 0 and d * d <= col_devices)
    return jax.shard_map(
        functools.partial(local, nx, groups, col_devices),
        mesh=mesh,
        in_specs=(
            P("chain", "col", None, None),
            P("chain", "col", None, None),
            P("chain", "col", None, None),
            P("chain", "col"),
            P("chain", "col"),
        ),
        out_specs=(P("chain", "col", None, None), P("chain", "col", None, None)),
        check_vma=False,
    )
```

```python
import functools

import jax
import jax.numpy as jnp
from jax import lax
from jax.experimental import pallas as pl
from jax.experimental.pallas import tpu as pltpu
from jax.sharding import PartitionSpec as P

MESH = pl.DeviceIdType.MESH
MIB = 1 << 20
PANELS = 2


def split(value):
    high = value.astype(jnp.bfloat16)
    low = (value - high.astype(jnp.float32)).astype(jnp.bfloat16)
    return high, low


def times_transposed(left, right):
    return lax.dot_general(left, right, (((1,), (1,)), ((), ())), preferred_element_type=jnp.float32)


def merge_kernel(pieces, rows_ref, cols_ref, factor_ref, high_ref, low_ref, held, total, arrived):
    tiles, size, _ = factor_ref.shape
    width = high_ref.shape[1] // size
    blocks = high_ref.shape[0] // size

    def fetch(i):
        span = pl.ds(pieces[i], pieces[i + 1] - pieces[i])
        return pltpu.make_async_copy(factor_ref.at[span], held.at[span], arrived.at[i])

    for i in range(len(pieces) - 1):
        fetch(i).start()

    def clear(block, carry):
        at = pl.ds(pl.multiple_of(block * size, size), size)
        total[at, :] = jnp.zeros((size, total.shape[1]), jnp.float32)
        return carry

    lax.fori_loop(0, blocks, clear, 0)

    def add(k, carry):
        row = pl.ds(pl.multiple_of(rows_ref[0, k] * size, size), size)
        col = pl.ds(pl.multiple_of(lax.rem(cols_ref[0, k], width) * size, size), size)
        total[row, col] += held[k]
        return carry

    for i in range(len(pieces) - 1):
        fetch(i).wait()
        lax.fori_loop(pieces[i], pieces[i + 1], add, 0)

    def finish(block, carry):
        at = pl.ds(pl.multiple_of(block * size, size), size)
        for c in range(width):
            cs = slice(c * size, (c + 1) * size)
            high, low = split(total[at, cs])
            high_ref[at, cs] = high
            low_ref[at, cs] = low
        return carry

    lax.fori_loop(0, blocks, finish, 0)


def merge(factor, rows, cols, row_tiles, col_tiles):
    tiles, size, _ = factor.shape
    pieces = list(range(0, tiles, 16)) + [tiles]
    shape = (row_tiles * size, col_tiles * size)
    whole = pl.BlockSpec(memory_space=pltpu.VMEM)
    scalars = pl.BlockSpec(memory_space=pltpu.SMEM)
    return pl.pallas_call(
        functools.partial(merge_kernel, pieces),
        out_shape=[pltpu.VMEM(shape, jnp.bfloat16)] * 2,
        in_specs=[scalars, scalars, pl.BlockSpec(memory_space=pltpu.HBM)],
        out_specs=[whole] * 2,
        scratch_shapes=[
            pltpu.VMEM(factor.shape, jnp.float32),
            pltpu.VMEM(shape, jnp.float32),
            pltpu.SemaphoreType.DMA((len(pieces) - 1,)),
        ],
        compiler_params=pltpu.CompilerParams(vmem_limit_bytes=40 * MIB),
    )(*(pltpu.with_memory_space_constraint(a, pltpu.HBM) for a in (rows, cols, factor)))


def chain_kernel(
    groups, nx, nz, panels,
    src_ref, inv_ref, high_ref, low_ref, solved_ref, leaving_ref,
    inv_high, inv_low, operand, own, xout, xin, zout, zin, zlast, bout, bin_, whole, fed_in,
    xsend, xrecv, zsend, zrecv, lrecv, bsend, brecv, fsend, frecv,
):
    g = lax.axis_index("chain")
    col = lax.axis_index("col")
    x = lax.rem(col, nx)
    z = lax.div(col, nx)
    per, sources, size = src_ref.shape
    wide = sources // panels
    last = g == groups - 1
    odd = lax.rem(g, 2) == 1
    even = jnp.logical_not(odd)
    keeps = odd | last
    near = jnp.logical_not(keeps)
    far = odd & jnp.logical_not(last)
    fed = even & (g > 0)

    def place(dx, dz):
        return lax.rem(z + dz, nz) * nx + lax.rem(x + dx, nx)

    barrier = pltpu.get_barrier_semaphore()

    def greet(chain, dx, dz):
        pl.semaphore_signal(barrier, inc=1, device_id=(chain, place(dx, dz)), device_id_type=MESH)

    for dx in range(1, nx):
        greet(g, dx, 0)

    @pl.when(odd)
    def _():
        for dz in range(nz):
            greet(g - 1, 0, dz)

    @pl.when(near)
    def _():
        for dz in range(nz):
            greet(g + 1, 0, dz)

    @pl.when(keeps)
    def _():
        for dz in range(1, nz):
            greet(g, 0, dz)

    @pl.when(far)
    def _():
        greet(g + 1, 0, 0)

    @pl.when(fed)
    def _():
        greet(g - 1, 0, 0)

    for t in range(per):
        inv_high[t], inv_low[t] = split(inv_ref[t])

    @pl.when(g == 0)
    def _():
        bout[...] = jnp.zeros(bout.shape, jnp.float32)

    awaited = (
        (nx - 1) + jnp.where(odd, nz, 0) + jnp.where(keeps, nz - 1, nz)
        + jnp.where(far, 1, 0) + jnp.where(fed, 1, 0)
    )
    pl.semaphore_wait(barrier, awaited)

    def x_copy(p, dx, dz):
        return pltpu.make_async_remote_copy(
            src_ref=xout.at[p, dx - 1, dz], dst_ref=xin.at[p, dx - 1, dz],
            send_sem=xsend.at[p, dx - 1, dz], recv_sem=xrecv.at[p, dx - 1, dz],
            device_id=(g, place(dx, 0)), device_id_type=MESH,
        )

    def z_copy(p, dz):
        return pltpu.make_async_remote_copy(
            src_ref=zout.at[p, dz], dst_ref=zin.at[p, dz],
            send_sem=zsend.at[p, dz], recv_sem=zrecv.at[p, dz],
            device_id=(g + 1, place(0, dz)), device_id_type=MESH,
        )

    def last_copy(p, dz):
        return pltpu.make_async_remote_copy(
            src_ref=zout.at[p, dz], dst_ref=zlast.at[p, dz],
            send_sem=zsend.at[p, dz], recv_sem=lrecv.at[p, dz],
            device_id=(g, place(0, dz)), device_id_type=MESH,
        )

    def back(p):
        return pltpu.make_async_remote_copy(
            src_ref=bout.at[p], dst_ref=bin_.at[p],
            send_sem=bsend.at[p], recv_sem=brecv.at[p],
            device_id=(g - 1, col), device_id_type=MESH,
        )

    def forward(p):
        return pltpu.make_async_remote_copy(
            src_ref=whole.at[p], dst_ref=fed_in.at[p],
            send_sem=fsend.at[p], recv_sem=frecv.at[p],
            device_id=(g + 1, col), device_id_type=MESH,
        )

    order = sorted(range(1, nz), key=lambda d: abs(2 * d - nz)) + [0]

    def chunk(dx, dz):
        rows = per * size
        at = pl.ds(pl.multiple_of(place(dx, dz) * rows, rows), rows)
        both = times_transposed(operand[...], high_ref[at, :])
        return both[:wide] + both[wide:] + times_transposed(operand[:wide, :], low_ref[at, :])

    def fill(dx, dz, store):
        result = chunk(dx, dz)
        for t in range(per):
            store[t] = result[:, t * size:(t + 1) * size]

    def first(p):
        @pl.when(odd)
        def _():
            for dz in range(nz):
                z_copy(p, dz).wait_recv()
            total = zin[p, 0]
            for dz in range(1, nz):
                total = total + zin[p, dz]
            bout[p] = total
            back(p).start()

        @pl.when(fed)
        def _():
            forward(p).wait_recv()
            bout[p] = fed_in[p]

        span = pl.ds(pl.multiple_of(p * wide, wide), wide)
        for t in range(per):
            right, rest = split(src_ref[t, span, :] - bout[p, t])
            both = times_transposed(jnp.concatenate([right, rest], axis=0), inv_high[t])
            current = both[:wide] + both[wide:] + times_transposed(right, inv_low[t])
            solved_ref[t, span, :] = current
            high, low = split(current)
            operand[:wide, t * size:(t + 1) * size] = high
            operand[wide:, t * size:(t + 1) * size] = low

        for dz in order:
            for dx in range(1, nx):
                fill(dx, dz, xout.at[p, dx - 1, dz])
                x_copy(p, dx, dz).start()
        for dz in order:
            fill(0, dz, own.at[p, dz])

    def second(p):
        for dz in order:
            for dx in range(1, nx):
                x_copy(p, dx, dz).wait_recv()
            part = own[p, dz]
            for dx in range(1, nx):
                part = part + xin[p, dx - 1, dz]
            zout[p, dz] = part

            @pl.when(near)
            def _():
                z_copy(p, dz).start()

            if dz > 0:
                @pl.when(keeps)
                def _():
                    last_copy(p, dz).start()

    def gather(p):
        total = zout[p, 0]
        for dz in range(1, nz):
            last_copy(p, dz).wait_recv()
            total = total + zlast[p, dz]
        whole[p] = total

    def tick(p, carry):
        first(p)
        second(p)

        @pl.when(far)
        def _():
            gather(p)
            forward(p).start()

        return carry

    lax.fori_loop(0, panels, tick, 0)

    def close(p, carry):
        span = pl.ds(pl.multiple_of(p * wide, wide), wide)

        @pl.when(last)
        def _():
            gather(p)

        @pl.when(keeps)
        def _():
            leaving_ref[:, span, :] = whole[p]
            for dz in range(1, nz):
                last_copy(p, dz).wait_send()

        @pl.when(far)
        def _():
            forward(p).wait_send()

        @pl.when(near)
        def _():
            back(p).wait_recv()
            leaving_ref[:, span, :] = bin_[p]
            for dz in range(nz):
                z_copy(p, dz).wait_send()

        for dz in order:
            for dx in range(1, nx):
                x_copy(p, dx, dz).wait_send()

        @pl.when(odd)
        def _():
            back(p).wait_send()

        return carry

    lax.fori_loop(0, panels, close, 0)


def local(nx, groups, col_devices, sources, diag_inverse, factor_tiles, tile_rows, tile_cols):
    per, panel_sources, size = sources.shape[1:]
    nz = col_devices // nx
    panels = PANELS if panel_sources % (16 * PANELS) == 0 else 1
    high, low = merge(factor_tiles[0], tile_rows, tile_cols, per * col_devices, per)
    block = (per, panel_sources, size)
    cut = (per, panel_sources // panels, size)
    whole = pl.BlockSpec(memory_space=pltpu.VMEM)
    dma = pltpu.SemaphoreType.DMA
    by_x = (panels, nx - 1, nz)
    by_z = (panels, nz)
    solved, leaving = pl.pallas_call(
        functools.partial(chain_kernel, groups, nx, nz, panels),
        out_shape=[jax.ShapeDtypeStruct(block, jnp.float32)] * 2,
        in_specs=[whole] * 4,
        out_specs=[whole] * 2,
        scratch_shapes=[
            pltpu.VMEM((per, size, size), jnp.bfloat16),
            pltpu.VMEM((per, size, size), jnp.bfloat16),
            pltpu.VMEM((2 * cut[1], per * size), jnp.bfloat16),
            pltpu.VMEM(by_z + cut, jnp.float32),
            pltpu.VMEM(by_x + cut, jnp.float32),
            pltpu.VMEM(by_x + cut, jnp.float32),
            pltpu.VMEM(by_z + cut, jnp.float32),
            pltpu.VMEM(by_z + cut, jnp.float32),
            pltpu.VMEM(by_z + cut, jnp.float32),
            pltpu.VMEM((panels,) + cut, jnp.float32),
            pltpu.VMEM((panels,) + cut, jnp.float32),
            pltpu.VMEM((panels,) + cut, jnp.float32),
            pltpu.VMEM((panels,) + cut, jnp.float32),
            dma(by_x),
            dma(by_x),
            dma(by_z),
            dma(by_z),
            dma(by_z),
            dma((panels,)),
            dma((panels,)),
            dma((panels,)),
            dma((panels,)),
        ],
        compiler_params=pltpu.CompilerParams(
            collective_id=0, has_side_effects=True, vmem_limit_bytes=36 * MIB
        ),
    )(sources[0], diag_inverse[0], high, low)
    return (solved[None], leaving[None])


def solution(mesh):
    groups, col_devices = mesh.shape["chain"], mesh.shape["col"]
    nx = max(d for d in range(1, col_devices + 1) if col_devices % d == 0 and d * d <= col_devices)
    return jax.shard_map(
        functools.partial(local, nx, groups, col_devices),
        mesh=mesh,
        in_specs=(
            P("chain", "col", None, None),
            P("chain", "col", None, None),
            P("chain", "col", None, None),
            P("chain", "col"),
            P("chain", "col"),
        ),
        out_specs=(P("chain", "col", None, None), P("chain", "col", None, None)),
        check_vma=False,
    )
```

```python
import functools

import jax
import jax.numpy as jnp
from jax import lax
from jax.experimental import pallas as pl
from jax.experimental.pallas import tpu as pltpu
from jax.sharding import PartitionSpec as P

MESH = pl.DeviceIdType.MESH
MIB = 1 << 20
PANELS = 2


def split(value):
    high = value.astype(jnp.bfloat16)
    low = (value - high.astype(jnp.float32)).astype(jnp.bfloat16)
    return high, low


def times_transposed(left, right):
    return lax.dot_general(left, right, (((1,), (1,)), ((), ())), preferred_element_type=jnp.float32)


def merge_kernel(pieces, rows_ref, cols_ref, factor_ref, total, held, arrived):
    tiles, size, _ = factor_ref.shape
    width = total.shape[1] // size
    blocks = total.shape[0] // size

    def fetch(i):
        span = pl.ds(pieces[i], pieces[i + 1] - pieces[i])
        return pltpu.make_async_copy(factor_ref.at[span], held.at[span], arrived.at[i])

    for i in range(len(pieces) - 1):
        fetch(i).start()

    def clear(block, carry):
        at = pl.ds(pl.multiple_of(block * size, size), size)
        total[at, :] = jnp.zeros((size, total.shape[1]), jnp.float32)
        return carry

    lax.fori_loop(0, blocks, clear, 0)

    def add(k, carry):
        row = pl.ds(pl.multiple_of(rows_ref[0, k] * size, size), size)
        col = pl.ds(pl.multiple_of(lax.rem(cols_ref[0, k], width) * size, size), size)
        total[row, col] += held[k]
        return carry

    for i in range(len(pieces) - 1):
        fetch(i).wait()
        lax.fori_loop(pieces[i], pieces[i + 1], add, 0)


def merge(factor, rows, cols, row_tiles, col_tiles):
    tiles, size, _ = factor.shape
    pieces = list(range(0, tiles, 16)) + [tiles]
    shape = (row_tiles * size, col_tiles * size)
    whole = pl.BlockSpec(memory_space=pltpu.VMEM)
    scalars = pl.BlockSpec(memory_space=pltpu.SMEM)
    return pl.pallas_call(
        functools.partial(merge_kernel, pieces),
        out_shape=pltpu.VMEM(shape, jnp.float32),
        in_specs=[scalars, scalars, pl.BlockSpec(memory_space=pltpu.HBM)],
        out_specs=whole,
        scratch_shapes=[
            pltpu.VMEM(factor.shape, jnp.float32),
            pltpu.SemaphoreType.DMA((len(pieces) - 1,)),
        ],
        compiler_params=pltpu.CompilerParams(vmem_limit_bytes=24 * MIB),
    )(*(pltpu.with_memory_space_constraint(a, pltpu.HBM) for a in (rows, cols, factor)))


def chain_kernel(
    groups, nx, nz, panels,
    src_ref, inv_ref, full_ref, solved_ref, leaving_ref,
    high_ref, low_ref, inv_high, inv_low, operand, own, xout, xin, zout, zin, zlast, bout, bin_,
    xsend, xrecv, zsend, zrecv, lrecv, bsend, brecv,
):
    g = lax.axis_index("chain")
    col = lax.axis_index("col")
    x = lax.rem(col, nx)
    z = lax.div(col, nx)
    per, sources, size = src_ref.shape
    wide = sources // panels
    last = g == groups - 1
    inner = jnp.logical_not(last)

    def place(dx, dz):
        return lax.rem(z + dz, nz) * nx + lax.rem(x + dx, nx)

    barrier = pltpu.get_barrier_semaphore()

    def greet(chain, dx, dz):
        pl.semaphore_signal(barrier, inc=1, device_id=(chain, place(dx, dz)), device_id_type=MESH)

    for dx in range(1, nx):
        greet(g, dx, 0)

    @pl.when(g > 0)
    def _():
        for dz in range(nz):
            greet(g - 1, 0, dz)

    @pl.when(inner)
    def _():
        for dz in range(nz):
            greet(g + 1, 0, dz)

    @pl.when(last)
    def _():
        for dz in range(1, nz):
            greet(g, 0, dz)

    for t in range(per):
        inv_high[t], inv_low[t] = split(inv_ref[t])

    @pl.when(g == 0)
    def _():
        bout[...] = jnp.zeros(bout.shape, jnp.float32)

    def cut_chunk(chunk_no):
        for t in range(per):
            at = pl.ds(pl.multiple_of((chunk_no * per + t) * size, size), size)
            high_ref[at, :], low_ref[at, :] = split(full_ref[at, :])

    awaited = (nx - 1) + jnp.where(g > 0, nz, 0) + jnp.where(last, nz - 1, nz)

    @pl.when(g > 0)
    def _():
        pl.semaphore_wait(barrier, awaited)

        def prepare(chunk_no, carry):
            cut_chunk(chunk_no)
            return carry

        lax.fori_loop(0, nx * nz, prepare, 0)

    def x_copy(p, dx, dz):
        return pltpu.make_async_remote_copy(
            src_ref=xout.at[p, dx - 1, dz], dst_ref=xin.at[p, dx - 1, dz],
            send_sem=xsend.at[p, dx - 1, dz], recv_sem=xrecv.at[p, dx - 1, dz],
            device_id=(g, place(dx, 0)), device_id_type=MESH,
        )

    def z_copy(p, dz):
        return pltpu.make_async_remote_copy(
            src_ref=zout.at[p, dz], dst_ref=zin.at[p, dz],
            send_sem=zsend.at[p, dz], recv_sem=zrecv.at[p, dz],
            device_id=(g + 1, place(0, dz)), device_id_type=MESH,
        )

    def last_copy(p, dz):
        return pltpu.make_async_remote_copy(
            src_ref=zout.at[p, dz], dst_ref=zlast.at[p, dz],
            send_sem=zsend.at[p, dz], recv_sem=lrecv.at[p, dz],
            device_id=(g, place(0, dz)), device_id_type=MESH,
        )

    def back(p):
        return pltpu.make_async_remote_copy(
            src_ref=bout.at[p], dst_ref=bin_.at[p],
            send_sem=bsend.at[p], recv_sem=brecv.at[p],
            device_id=(g - 1, col), device_id_type=MESH,
        )

    order = sorted(range(1, nz), key=lambda d: abs(2 * d - nz)) + [0]

    def chunk(dx, dz):
        rows = per * size
        at = pl.ds(pl.multiple_of(place(dx, dz) * rows, rows), rows)
        both = times_transposed(operand[...], high_ref[at, :])
        return both[:wide] + both[wide:] + times_transposed(operand[:wide, :], low_ref[at, :])

    def early(p, dx, dz):
        @pl.when((g == 0) & (p == 0))
        def _():
            cut_chunk(place(dx, dz))

    def first(p):
        @pl.when(g > 0)
        def _():
            for dz in range(nz):
                z_copy(p, dz).wait_recv()
            total = zin[p, 0]
            for dz in range(1, nz):
                total = total + zin[p, dz]
            bout[p] = total
            back(p).start()

        span = pl.ds(pl.multiple_of(p * wide, wide), wide)
        for t in range(per):
            right, rest = split(src_ref[t, span, :] - bout[p, t])
            both = times_transposed(jnp.concatenate([right, rest], axis=0), inv_high[t])
            current = both[:wide] + both[wide:] + times_transposed(right, inv_low[t])
            solved_ref[t, span, :] = current
            high, low = split(current)
            operand[:wide, t * size:(t + 1) * size] = high
            operand[wide:, t * size:(t + 1) * size] = low

        for dz in order:
            for dx in range(1, nx):
                early(p, dx, dz)
                result = chunk(dx, dz)
                for t in range(per):
                    xout[p, dx - 1, dz, t] = result[:, t * size:(t + 1) * size]
                if dz == order[0] and dx == 1:
                    @pl.when((g == 0) & (p == 0))
                    def _():
                        pl.semaphore_wait(barrier, awaited)

                x_copy(p, dx, dz).start()
        for dz in order:
            early(p, 0, dz)
            result = chunk(0, dz)
            for t in range(per):
                own[p, dz, t] = result[:, t * size:(t + 1) * size]

    def second(p):
        for dz in order:
            for dx in range(1, nx):
                x_copy(p, dx, dz).wait_recv()
            part = own[p, dz]
            for dx in range(1, nx):
                part = part + xin[p, dx - 1, dz]
            zout[p, dz] = part

            @pl.when(inner)
            def _():
                z_copy(p, dz).start()

            if dz > 0:
                @pl.when(last)
                def _():
                    last_copy(p, dz).start()

    def tick(p, carry):
        first(p)
        second(p)
        return carry

    lax.fori_loop(0, panels, tick, 0)

    def close(p, carry):
        span = pl.ds(pl.multiple_of(p * wide, wide), wide)

        @pl.when(last)
        def _():
            total = zout[p, 0]
            for dz in range(1, nz):
                last_copy(p, dz).wait_recv()
                total = total + zlast[p, dz]
            leaving_ref[:, span, :] = total
            for dz in range(1, nz):
                last_copy(p, dz).wait_send()

        @pl.when(inner)
        def _():
            back(p).wait_recv()
            leaving_ref[:, span, :] = bin_[p]
            for dz in range(nz):
                z_copy(p, dz).wait_send()

        for dz in order:
            for dx in range(1, nx):
                x_copy(p, dx, dz).wait_send()

        @pl.when(g > 0)
        def _():
            back(p).wait_send()

        return carry

    lax.fori_loop(0, panels, close, 0)


def local(nx, groups, col_devices, sources, diag_inverse, factor_tiles, tile_rows, tile_cols):
    per, panel_sources, size = sources.shape[1:]
    nz = col_devices // nx
    panels = PANELS if panel_sources % (16 * PANELS) == 0 else 1
    full = merge(factor_tiles[0], tile_rows, tile_cols, per * col_devices, per)
    block = (per, panel_sources, size)
    cut = (per, panel_sources // panels, size)
    whole = pl.BlockSpec(memory_space=pltpu.VMEM)
    dma = pltpu.SemaphoreType.DMA
    by_x = (panels, nx - 1, nz)
    by_z = (panels, nz)
    solved, leaving = pl.pallas_call(
        functools.partial(chain_kernel, groups, nx, nz, panels),
        out_shape=[jax.ShapeDtypeStruct(block, jnp.float32)] * 2,
        in_specs=[whole] * 3,
        out_specs=[whole] * 2,
        scratch_shapes=[
            pltpu.VMEM(full.shape, jnp.bfloat16),
            pltpu.VMEM(full.shape, jnp.bfloat16),
            pltpu.VMEM((per, size, size), jnp.bfloat16),
            pltpu.VMEM((per, size, size), jnp.bfloat16),
            pltpu.VMEM((2 * cut[1], per * size), jnp.bfloat16),
            pltpu.VMEM(by_z + cut, jnp.float32),
            pltpu.VMEM(by_x + cut, jnp.float32),
            pltpu.VMEM(by_x + cut, jnp.float32),
            pltpu.VMEM(by_z + cut, jnp.float32),
            pltpu.VMEM(by_z + cut, jnp.float32),
            pltpu.VMEM(by_z + cut, jnp.float32),
            pltpu.VMEM((panels,) + cut, jnp.float32),
            pltpu.VMEM((panels,) + cut, jnp.float32),
            dma(by_x),
            dma(by_x),
            dma(by_z),
            dma(by_z),
            dma(by_z),
            dma((panels,)),
            dma((panels,)),
        ],
        compiler_params=pltpu.CompilerParams(
            collective_id=0, has_side_effects=True, vmem_limit_bytes=36 * MIB
        ),
    )(sources[0], diag_inverse[0], full)
    return (solved[None], leaving[None])


def solution(mesh):
    groups, col_devices = mesh.shape["chain"], mesh.shape["col"]
    nx = max(d for d in range(1, col_devices + 1) if col_devices % d == 0 and d * d <= col_devices)
    return jax.shard_map(
        functools.partial(local, nx, groups, col_devices),
        mesh=mesh,
        in_specs=(
            P("chain", "col", None, None),
            P("chain", "col", None, None),
            P("chain", "col", None, None),
            P("chain", "col"),
            P("chain", "col"),
        ),
        out_specs=(P("chain", "col", None, None), P("chain", "col", None, None)),
        check_vma=False,
    )
```

```python
import functools

import jax
import jax.numpy as jnp
from jax import lax
from jax.experimental import pallas as pl
from jax.experimental.pallas import tpu as pltpu
from jax.sharding import PartitionSpec as P

MESH = pl.DeviceIdType.MESH
MIB = 1 << 20
PANELS = 2


def split(value):
    high = value.astype(jnp.bfloat16)
    low = (value - high.astype(jnp.float32)).astype(jnp.bfloat16)
    return high, low


def times_transposed(left, right):
    return lax.dot_general(left, right, (((1,), (1,)), ((), ())), preferred_element_type=jnp.float32)


def merge_kernel(pieces, rows_ref, cols_ref, factor_ref, total, held, arrived):
    tiles, size, _ = factor_ref.shape
    width = total.shape[1] // size
    blocks = total.shape[0] // size

    start = lax.axis_index("col") * width

    def fetch(i):
        span = pl.ds(pieces[i], pieces[i + 1] - pieces[i])
        return pltpu.make_async_copy(factor_ref.at[span], held.at[span], arrived.at[i])

    for i in range(len(pieces) - 1):
        fetch(i).start()

    def clear(block, carry):
        at = pl.ds(pl.multiple_of(block * size, size), size)
        total[at, :] = jnp.zeros((size, total.shape[1]), jnp.float32)
        return carry

    lax.fori_loop(0, blocks, clear, 0)

    def add(k, carry):
        row = pl.ds(pl.multiple_of(rows_ref[0, k] * size, size), size)
        col = pl.ds(pl.multiple_of((cols_ref[0, k] - start) * size, size), size)
        total[row, col] += held[k]
        return carry

    for i in range(len(pieces) - 1):
        fetch(i).wait()
        lax.fori_loop(pieces[i], pieces[i + 1], add, 0, unroll=2)


def merge(factor, rows, cols, row_tiles, col_tiles):
    tiles, size, _ = factor.shape
    pieces = list(range(0, tiles, 16)) + [tiles]
    shape = (row_tiles * size, col_tiles * size)
    whole = pl.BlockSpec(memory_space=pltpu.VMEM)
    scalars = pl.BlockSpec(memory_space=pltpu.SMEM)
    return pl.pallas_call(
        functools.partial(merge_kernel, pieces),
        out_shape=pltpu.VMEM(shape, jnp.float32),
        in_specs=[scalars, scalars, pl.BlockSpec(memory_space=pltpu.HBM)],
        out_specs=whole,
        scratch_shapes=[
            pltpu.VMEM(factor.shape, jnp.float32),
            pltpu.SemaphoreType.DMA((len(pieces) - 1,)),
        ],
        compiler_params=pltpu.CompilerParams(vmem_limit_bytes=24 * MIB),
    )(*(pltpu.with_memory_space_constraint(a, pltpu.HBM) for a in (rows, cols, factor)))


def chain_kernel(
    groups, nx, nz, panels,
    src_ref, inv_ref, full_ref, solved_ref, leaving_ref,
    high_ref, low_ref, inv_high, inv_low, operand, own, xout, xin, zout, zin, zlast, bout, bin_,
    xsend, xrecv, zsend, zrecv, lrecv, bsend, brecv,
):
    g = lax.axis_index("chain")
    col = lax.axis_index("col")
    x = lax.rem(col, nx)
    z = lax.div(col, nx)
    per, sources, size = src_ref.shape
    wide = sources // panels
    last = g == groups - 1
    inner = jnp.logical_not(last)

    def place(dx, dz):
        return lax.rem(z + dz, nz) * nx + lax.rem(x + dx, nx)

    barrier = pltpu.get_barrier_semaphore()

    def greet(chain, dx, dz):
        pl.semaphore_signal(barrier, inc=1, device_id=(chain, place(dx, dz)), device_id_type=MESH)

    for dx in range(1, nx):
        greet(g, dx, 0)

    @pl.when(g > 0)
    def _():
        for dz in range(nz):
            greet(g - 1, 0, dz)

    @pl.when(inner)
    def _():
        for dz in range(nz):
            greet(g + 1, 0, dz)

    @pl.when(last)
    def _():
        for dz in range(1, nz):
            greet(g, 0, dz)

    for t in range(per):
        inv_high[t], inv_low[t] = split(inv_ref[t])

    @pl.when(g == 0)
    def _():
        bout[...] = jnp.zeros(bout.shape, jnp.float32)

    def cut_chunk(chunk_no):
        for t in range(per):
            at = pl.ds(pl.multiple_of((chunk_no * per + t) * size, size), size)
            high_ref[at, :], low_ref[at, :] = split(full_ref[at, :])

    awaited = (nx - 1) + jnp.where(g > 0, nz, 0) + jnp.where(last, nz - 1, nz)

    @pl.when(g > 0)
    def _():
        pl.semaphore_wait(barrier, awaited)

        def prepare(chunk_no, carry):
            cut_chunk(chunk_no)
            return carry

        lax.fori_loop(0, nx * nz, prepare, 0)

    def x_copy(p, dx, dz):
        return pltpu.make_async_remote_copy(
            src_ref=xout.at[p, dx - 1, dz], dst_ref=xin.at[p, dx - 1, dz],
            send_sem=xsend.at[p, dx - 1, dz], recv_sem=xrecv.at[p, dx - 1, dz],
            device_id=(g, place(dx, 0)), device_id_type=MESH,
        )

    def z_copy(p, dz):
        return pltpu.make_async_remote_copy(
            src_ref=zout.at[p, dz], dst_ref=zin.at[p, dz],
            send_sem=zsend.at[p, dz], recv_sem=zrecv.at[p, dz],
            device_id=(g + 1, place(0, dz)), device_id_type=MESH,
        )

    def last_copy(p, dz):
        return pltpu.make_async_remote_copy(
            src_ref=zout.at[p, dz], dst_ref=zlast.at[p, dz],
            send_sem=zsend.at[p, dz], recv_sem=lrecv.at[p, dz],
            device_id=(g, place(0, dz)), device_id_type=MESH,
        )

    def back(p):
        return pltpu.make_async_remote_copy(
            src_ref=bout.at[p], dst_ref=bin_.at[p],
            send_sem=bsend.at[p], recv_sem=brecv.at[p],
            device_id=(g - 1, col), device_id_type=MESH,
        )

    order = sorted(range(1, nz), key=lambda d: abs(2 * d - nz)) + [0]

    def chunk(dx, dz):
        rows = per * size
        at = pl.ds(pl.multiple_of(place(dx, dz) * rows, rows), rows)
        both = times_transposed(operand[...], high_ref[at, :])
        return both[:wide] + both[wide:] + times_transposed(operand[:wide, :], low_ref[at, :])

    def early(p, dx, dz):
        @pl.when((g == 0) & (p == 0))
        def _():
            cut_chunk(place(dx, dz))

    def first(p):
        @pl.when(g > 0)
        def _():
            for dz in range(nz):
                z_copy(p, dz).wait_recv()
            total = zin[p, 0]
            for dz in range(1, nz):
                total = total + zin[p, dz]
            bout[p] = total

        span = pl.ds(pl.multiple_of(p * wide, wide), wide)
        for t in range(per):
            right, rest = split(src_ref[t, span, :] - bout[p, t])
            both = times_transposed(jnp.concatenate([right, rest], axis=0), inv_high[t])
            current = both[:wide] + both[wide:] + times_transposed(right, inv_low[t])
            solved_ref[t, span, :] = current
            high, low = split(current)
            operand[:wide, t * size:(t + 1) * size] = high
            operand[wide:, t * size:(t + 1) * size] = low

        for dz in order:
            for dx in range(1, nx):
                early(p, dx, dz)
                result = chunk(dx, dz)
                for t in range(per):
                    xout[p, dx - 1, dz, t] = result[:, t * size:(t + 1) * size]
                if dz == order[0] and dx == 1:
                    @pl.when((g == 0) & (p == 0))
                    def _():
                        pl.semaphore_wait(barrier, awaited)

                x_copy(p, dx, dz).start()
        for dz in order:
            early(p, 0, dz)
            result = chunk(0, dz)
            for t in range(per):
                own[p, dz, t] = result[:, t * size:(t + 1) * size]

        @pl.when(g > 0)
        def _():
            back(p).start()

    def second(p):
        for dz in order:
            for dx in range(1, nx):
                x_copy(p, dx, dz).wait_recv()
            part = own[p, dz]
            for dx in range(1, nx):
                part = part + xin[p, dx - 1, dz]
            zout[p, dz] = part

            @pl.when(inner)
            def _():
                z_copy(p, dz).start()

            if dz > 0:
                @pl.when(last)
                def _():
                    last_copy(p, dz).start()

    def tick(p, carry):
        first(p)
        second(p)
        return carry

    lax.fori_loop(0, panels, tick, 0)

    def close(p, carry):
        span = pl.ds(pl.multiple_of(p * wide, wide), wide)

        @pl.when(last)
        def _():
            total = zout[p, 0]
            for dz in range(1, nz):
                last_copy(p, dz).wait_recv()
                total = total + zlast[p, dz]
            leaving_ref[:, span, :] = total
            for dz in range(1, nz):
                last_copy(p, dz).wait_send()

        @pl.when(inner)
        def _():
            back(p).wait_recv()
            leaving_ref[:, span, :] = bin_[p]
            for dz in range(nz):
                z_copy(p, dz).wait_send()

        for dz in order:
            for dx in range(1, nx):
                x_copy(p, dx, dz).wait_send()

        @pl.when(g > 0)
        def _():
            back(p).wait_send()

        return carry

    lax.fori_loop(0, panels, close, 0)


def local(nx, groups, col_devices, sources, diag_inverse, factor_tiles, tile_rows, tile_cols):
    per, panel_sources, size = sources.shape[1:]
    nz = col_devices // nx
    panels = PANELS if panel_sources % (16 * PANELS) == 0 else 1
    full = merge(factor_tiles[0], tile_rows, tile_cols, per * col_devices, per)
    block = (per, panel_sources, size)
    cut = (per, panel_sources // panels, size)
    whole = pl.BlockSpec(memory_space=pltpu.VMEM)
    dma = pltpu.SemaphoreType.DMA
    by_x = (panels, nx - 1, nz)
    by_z = (panels, nz)
    solved, leaving = pl.pallas_call(
        functools.partial(chain_kernel, groups, nx, nz, panels),
        out_shape=[jax.ShapeDtypeStruct(block, jnp.float32)] * 2,
        in_specs=[whole] * 3,
        out_specs=[whole] * 2,
        scratch_shapes=[
            pltpu.VMEM(full.shape, jnp.bfloat16),
            pltpu.VMEM(full.shape, jnp.bfloat16),
            pltpu.VMEM((per, size, size), jnp.bfloat16),
            pltpu.VMEM((per, size, size), jnp.bfloat16),
            pltpu.VMEM((2 * cut[1], per * size), jnp.bfloat16),
            pltpu.VMEM(by_z + cut, jnp.float32),
            pltpu.VMEM(by_x + cut, jnp.float32),
            pltpu.VMEM(by_x + cut, jnp.float32),
            pltpu.VMEM(by_z + cut, jnp.float32),
            pltpu.VMEM(by_z + cut, jnp.float32),
            pltpu.VMEM(by_z + cut, jnp.float32),
            pltpu.VMEM((panels,) + cut, jnp.float32),
            pltpu.VMEM((panels,) + cut, jnp.float32),
            dma(by_x),
            dma(by_x),
            dma(by_z),
            dma(by_z),
            dma(by_z),
            dma((panels,)),
            dma((panels,)),
        ],
        compiler_params=pltpu.CompilerParams(
            collective_id=0, has_side_effects=True, vmem_limit_bytes=36 * MIB
        ),
    )(sources[0], diag_inverse[0], full)
    return (solved[None], leaving[None])


def solution(mesh):
    groups, col_devices = mesh.shape["chain"], mesh.shape["col"]
    nx = max(d for d in range(1, col_devices + 1) if col_devices % d == 0 and d * d <= col_devices)
    return jax.shard_map(
        functools.partial(local, nx, groups, col_devices),
        mesh=mesh,
        in_specs=(
            P("chain", "col", None, None),
            P("chain", "col", None, None),
            P("chain", "col", None, None),
            P("chain", "col"),
            P("chain", "col"),
        ),
        out_specs=(P("chain", "col", None, None), P("chain", "col", None, None)),
        check_vma=False,
    )
```
